32 devices in a mesh: req: 8 (over z, y), tp: 4 (over x, core).
Axes of the slice: x: 2, y: 2, z: 4, core: 2. Of those that a mesh axis runs over, the one named last changes fastest.
Arguments:
- tokens: bfloat16 [32, 1024], P('req'), may hold values from -6 to 6
- deal: int32 [32], replicated, may hold values from 0 to 31, each once
- self_len: int32 [32], P('req'), may hold values from 1 to 512, 2048 in all
- enc_len: int32 [32], P('req'), may hold values from 1 to 256, 4096 in all
- self_cache: bfloat16 [32, 512, 2, 1024], P('req', None, None, 'tp'), may hold values from -320 to 320
- cross_cache: bfloat16 [32, 256, 2, 1024], P('req', None, None, 'tp'), may hold values from -320 to 320
- w_qkv: bfloat16 [1024, 3, 1024], P(None, None, 'tp'), may hold values from -0.1875 to 0.1875
- b_qkv: bfloat16 [3, 1024], P(None, 'tp'), may hold values from -3 to 3
- w_out: bfloat16 [1024, 1024], P('tp'), may hold values from -0.1875 to 0.1875
- b_out: bfloat16 [1024], replicated, may hold values from -3 to 3
- ln1_gain: bfloat16 [1024], replicated, may hold values from 0.25 to 1.75
- ln1_bias: bfloat16 [1024], replicated, may hold values from -2 to 2
- w_cq: bfloat16 [1024, 1024], P(None, 'tp'), may hold values from -0.1875 to 0.1875
- b_cq: bfloat16 [1024], P('tp'), may hold values from -3 to 3
- w_cout: bfloat16 [1024, 1024], P('tp'), may hold values from -0.1875 to 0.1875
- b_cout: bfloat16 [1024], replicated, may hold values from -3 to 3
- ln2_gain: bfloat16 [1024], replicated, may hold values from 0.25 to 1.75
- ln2_bias: bfloat16 [1024], replicated, may hold values from -2 to 2
- w_up: bfloat16 [1024, 4096], P(None, 'tp'), may hold values from -0.1875 to 0.1875
- b_up: bfloat16 [4096], P('tp'), may hold values from -3 to 3
- w_down: bfloat16 [4096, 1024], P('tp'), may hold values from -0.09375 to 0.09375
- b_down: bfloat16 [1024], replicated, may hold values from -3 to 3
- ln3_gain: bfloat16 [1024], replicated, may hold values from 0.25 to 1.75
- ln3_bias: bfloat16 [1024], replicated, may hold values from -2 to 2
Outputs:
- result: bfloat16 [32, 1024], P('req')
The draws below stay inside these ranges and needn't reach their ends.
Inputs may be any that keep to these rules, and one draw needn't show every extreme that they name: deal is a permutation of the requests: slot s holds the caches of request deal[s].
All inputs are finite; a program needn't handle non-finite values. No bound on the sum of `self_len` or of `enc_len` on one device may be relied on, other than what follows from the above.
Results may differ from the reference program's by a relative error of at most 0.039.
Values may be sent and summed in bfloat16 or wider, within the bound.
No kernel may reach another device: no remote copies, remote signals or barrier semaphores. Data moves between devices by JAX's collectives and lax.ppermute only.
A program may use at most 64 MiB of HBM per device.

```python
import math
import jax
import jax.numpy as jnp
import numpy as np
from jax import lax

HEADS = 16
HEAD_DIM = 64
D = 1024
FF = 4096
SELF_MAX = 512
ENC_MAX = 256
REQS = 32


def draw_cache(key, length):
    entries = jax.random.truncated_normal(key, -5.0, 5.0, (REQS, length, 2, D), jnp.float32)
    return entries


def draw_self_cache(key, part):
    return draw_cache(jax.random.fold_in(key, 11), SELF_MAX).astype(jnp.bfloat16)


def draw_cross_cache(key, part):
    return draw_cache(jax.random.fold_in(key, 13), ENC_MAX).astype(jnp.bfloat16)


def levels(key, extent, shards, smallest, high):
    def one(axis_at, shards_of):
        heights = jax.random.uniform(jax.random.fold_in(jax.random.fold_in(key, 6), axis_at), (shards_of,), jnp.float32, smallest / len(shards), high / len(shards))
        return jnp.repeat(jnp.exp(heights), extent[axis_at] // shards_of).reshape((-1,) + (1,) * (len(extent) - axis_at - 1))

    loudness = one(*shards[0])
    for cut in shards[1:]:
        loudness = loudness * one(*cut)
    return loudness


def split_up(number_of, total, most, skew):
    portions = [(1 << 20) // math.isqrt(grade ** skew) + 1 for grade in range(2, number_of + 1)]
    spare, given = total - most - (number_of - 1), [1] * (number_of - 1)
    while spare > 0:
        movable = [i for i in range(number_of - 1) if given[i] < most]
        whole, remaining = sum([portions[i] for i in movable]), spare
        for i in movable:
            addition = min(most - given[i], max(1, remaining * portions[i] // whole), spare)
            given[i] = given[i] + addition
            spare = spare - addition
    return np.array([most] + given)


def ragged_sizes(own_key, amount, total, limit, skew):
    if amount == 2:
        one = jax.random.randint(own_key, (), max(1, total - limit), min(limit, total - 1) + 1)
        return jnp.stack([one, total - one])
    lengths = jnp.asarray(split_up(amount, total, limit, skew), jnp.int32)
    twos = (amount - 1) // 2
    donor, sink = lengths[1:1 + 2 * twos:2], lengths[2:2 + 2 * twos:2]
    room = jnp.minimum(donor - 1, limit - sink)
    shifted = jax.random.randint(jax.random.fold_in(own_key, 1), (twos,), 0, 1 << 20) % (room + 1)
    lengths = lengths.at[1:1 + 2 * twos:2].set(donor - shifted).at[2:2 + 2 * twos:2].set(sink + shifted)
    return lengths[jax.random.permutation(jax.random.fold_in(own_key, 2), amount)]


def scatter_about(rng, extent, width, limit, split=(), kind=jnp.bfloat16):
    result = width * jax.random.normal(rng, extent, jnp.float32)
    if split:
        result = result * levels(rng, extent, split, -0.22, 0.18)
    return jnp.clip(result, -limit, limit).astype(kind)


def setup_inputs(seed: int = 0) -> dict:
    splits = jax.random.split(jax.random.key(seed), 25)
    return {
        "tokens": scatter_about(splits[0], (REQS, D), 1.0, 6.0, ((0, 8),)),
        "deal": jax.random.permutation(splits[1], REQS).astype(jnp.int32),
        "self_len": ragged_sizes(splits[2], REQS, REQS * SELF_MAX // 8, SELF_MAX, 2).astype(jnp.int32),
        "enc_len": ragged_sizes(splits[3], REQS, REQS * ENC_MAX // 2, ENC_MAX, 1).astype(jnp.int32),
        "self_cache": draw_self_cache(jax.random.fold_in(splits[24], 71), 0),
        "cross_cache": draw_cross_cache(jax.random.fold_in(splits[24], 71), 0),
        "w_qkv": scatter_about(splits[6], (D, 3, D), D ** -0.5, 0.1875, ((2, 4),)),
        "b_qkv": scatter_about(splits[7], (3, D), 0.5, 3.0, ((1, 4),)),
        "w_out": scatter_about(splits[8], (D, D), D ** -0.5, 0.1875, ((0, 4),)),
        "b_out": scatter_about(splits[9], (D,), 0.5, 3.0),
        "ln1_gain": jnp.clip(1.0 + 0.15 * jax.random.normal(splits[10], (D,), jnp.float32), 0.25, 1.75).astype(jnp.bfloat16),
        "ln1_bias": scatter_about(splits[11], (D,), 0.3, 2.0),
        "w_cq": scatter_about(splits[12], (D, D), D ** -0.5, 0.1875, ((1, 4),)),
        "b_cq": scatter_about(splits[13], (D,), 0.5, 3.0, ((0, 4),)),
        "w_cout": scatter_about(splits[14], (D, D), D ** -0.5, 0.1875, ((0, 4),)),
        "b_cout": scatter_about(splits[15], (D,), 0.5, 3.0),
        "ln2_gain": jnp.clip(1.0 + 0.15 * jax.random.normal(splits[16], (D,), jnp.float32), 0.25, 1.75).astype(jnp.bfloat16),
        "ln2_bias": scatter_about(splits[17], (D,), 0.3, 2.0),
        "w_up": scatter_about(splits[18], (D, FF), D ** -0.5, 0.1875, ((1, 4),)),
        "b_up": scatter_about(splits[19], (FF,), 0.5, 3.0, ((0, 4),)),
        "w_down": scatter_about(splits[20], (FF, D), FF ** -0.5, 0.09375, ((0, 4),)),
        "b_down": scatter_about(splits[21], (D,), 0.5, 3.0),
        "ln3_gain": jnp.clip(1.0 + 0.15 * jax.random.normal(splits[22], (D,), jnp.float32), 0.25, 1.75).astype(jnp.bfloat16),
        "ln3_bias": scatter_about(splits[23], (D,), 0.3, 2.0),
    }


def norm_rows(total, gain, beta):
    mean = lax.optimization_barrier(jnp.mean(total, axis=-1, keepdims=True))
    centered = total - mean
    var = lax.optimization_barrier(jnp.mean(centered * centered, axis=-1, keepdims=True))
    return centered / jnp.sqrt(var + 1e-05) * gain.astype(jnp.float32) + beta.astype(jnp.float32)

def reference(tokens, deal, self_len, enc_len, self_cache, cross_cache, w_qkv, b_qkv, w_out, b_out, ln1_gain, ln1_bias, w_cq, b_cq, w_cout, b_cout, ln2_gain, ln2_bias, w_up, b_up, w_down, b_down, ln3_gain, ln3_bias):
    f32 = jnp.float32
    bf = jnp.bfloat16
    scale = HEAD_DIM ** (-0.5)
    x = tokens[deal]
    qkv = (jnp.einsum('nd,dke->nke', x.astype(f32), w_qkv.astype(f32)) + b_qkv.astype(f32)).astype(bf)

    def self_one(item):
        triple, cache, length = item
        query = triple[0].astype(f32).reshape(HEADS, HEAD_DIM)
        new_key = triple[1].astype(f32).reshape(HEADS, HEAD_DIM)
        new_value = triple[2].astype(f32).reshape(HEADS, HEAD_DIM)
        keys = cache[:, 0, :].astype(f32).reshape(SELF_MAX, HEADS, HEAD_DIM)
        values = cache[:, 1, :].astype(f32).reshape(SELF_MAX, HEADS, HEAD_DIM)
        scores = jnp.einsum('he,mhe->hm', query, keys) * scale
        fresh = lax.optimization_barrier(jnp.sum(query * new_key, axis=-1)) * scale
        valid = jnp.arange(SELF_MAX, dtype=jnp.int32)[None, :] < length
        scores = jnp.where(valid, scores, -jnp.inf)
        top = jnp.maximum(lax.optimization_barrier(jnp.max(scores, axis=-1)), fresh)
        expo = jnp.exp(scores - top[:, None])
        expn = jnp.exp(fresh - top)
        total = lax.optimization_barrier(jnp.sum(expo, axis=-1)) + expn
        weights = (expo / total[:, None]).astype(bf).astype(f32)
        wnew = (expn / total).astype(bf).astype(f32)
        ctx = jnp.einsum('hm,mhe->he', weights, values) + wnew[:, None] * new_value
        return ctx.reshape(D).astype(bf)
    ctx = lax.map(self_one, (qkv, self_cache, self_len))
    h1 = norm_rows(jnp.dot(ctx, w_out, preferred_element_type=f32) + b_out.astype(f32) + x.astype(f32), ln1_gain, ln1_bias).astype(bf)
    cq = (jnp.dot(h1, w_cq, preferred_element_type=f32) + b_cq.astype(f32)).astype(bf)

    def cross_one(item):
        query, cache, length = item
        query = query.astype(f32).reshape(HEADS, HEAD_DIM)
        keys = cache[:, 0, :].astype(f32).reshape(ENC_MAX, HEADS, HEAD_DIM)
        values = cache[:, 1, :].astype(f32).reshape(ENC_MAX, HEADS, HEAD_DIM)
        scores = jnp.einsum('he,mhe->hm', query, keys) * scale
        valid = jnp.arange(ENC_MAX, dtype=jnp.int32)[None, :] < length
        scores = jnp.where(valid, scores, -jnp.inf)
        top = lax.optimization_barrier(jnp.max(scores, axis=-1))
        expo = jnp.exp(scores - top[:, None])
        weights = (expo / lax.optimization_barrier(jnp.sum(expo, axis=-1))[:, None]).astype(bf).astype(f32)
        ctx = jnp.einsum('hm,mhe->he', weights, values)
        return ctx.reshape(D).astype(bf)
    ctx2 = lax.map(cross_one, (cq, cross_cache, enc_len))
    h2 = norm_rows(jnp.dot(ctx2, w_cout, preferred_element_type=f32) + b_cout.astype(f32) + h1.astype(f32), ln2_gain, ln2_bias).astype(bf)
    act = jax.nn.gelu(jnp.dot(h2, w_up, preferred_element_type=f32) + b_up.astype(f32), approximate=False).astype(bf)
    y = norm_rows(jnp.dot(act, w_down, preferred_element_type=f32) + b_down.astype(f32) + h2.astype(f32), ln3_gain, ln3_bias).astype(bf)
    return jnp.zeros_like(y).at[deal].set(y)
```

```python
import functools

import jax
import jax.numpy as jnp
from jax import lax
from jax.experimental import pallas as pl
from jax.experimental.pallas import tpu as pltpu
from jax.sharding import PartitionSpec as P

HEAD_DIM = 64
LANES = 128
EPS = 1e-05
MASKED = -1e30
SPARE_FLOPS = 10**10
f32 = jnp.float32
bf16 = jnp.bfloat16


def norm_rows(total, gain, beta):
    mean = jnp.mean(total, axis=-1, keepdims=True)
    centered = total - mean
    var = jnp.mean(centered * centered, axis=-1, keepdims=True)
    return centered / jnp.sqrt(var + EPS) * gain + beta


def round_rows(value):
    return value.astype(bf16).astype(f32)


def dot(a, b):
    return jnp.dot(a.astype(bf16), b, preferred_element_type=f32)


def dot_t(a, b):
    return lax.dot_general(
        a.astype(bf16), b, (((1,), (1,)), ((), ())), preferred_element_type=f32
    )


def pad_rows(value, rows):
    return jnp.concatenate(
        [value, jnp.zeros((rows - value.shape[0], value.shape[1]), value.dtype)], axis=0
    )


def head_rows(vec, slot, heads, first):
    return jnp.where(first, vec[slot : slot + 1], vec[slot + 1 : slot + 2])


def attend(query, cache, lens, heads, fresh_key=None, fresh_value=None):
    slots, _, span, width = cache.shape
    pair = 2 * heads
    scale = HEAD_DIM ** (-0.5)
    row = lax.broadcasted_iota(jnp.int32, (pair, width), 0)
    lane = lax.broadcasted_iota(jnp.int32, (pair, width), 1)
    first = row < heads
    own = (lane // HEAD_DIM) == jnp.where(first, row, row - heads)
    first_col = lax.broadcasted_iota(jnp.int32, (pair, span), 0) < heads
    position = lax.broadcasted_iota(jnp.int32, (pair, span), 1)
    rows = []
    for slot in range(0, slots, 2):
        q = jnp.where(own, head_rows(query, slot, heads, first) * scale, 0.0)
        raw = [dot_t(q, cache[slot + i, 0]) for i in range(2)]
        length = jnp.where(first_col, lens[slot], lens[slot + 1])
        scores = jnp.where(position < length, jnp.where(first_col, raw[0], raw[1]), MASKED)
        top = jnp.max(scores, axis=-1, keepdims=True)
        if fresh_key is not None:
            k_new = head_rows(fresh_key, slot, heads, first)
            v_new = head_rows(fresh_value, slot, heads, first)
            fresh = jnp.sum(q * k_new, axis=-1, keepdims=True)
            top = jnp.maximum(top, fresh)
        expo = jnp.exp(scores - top)
        total = jnp.sum(expo, axis=-1, keepdims=True)
        if fresh_key is not None:
            expn = jnp.exp(fresh - top)
            total = total + expn
        share = 1.0 / total
        weights = expo * share
        out = [dot(weights, cache[slot + i, 1]) for i in range(2)]
        ctx = jnp.where(first, out[0], out[1])
        if fresh_key is not None:
            ctx = ctx + round_rows(expn * share) * v_new
        ctx = jnp.where(own, round_rows(ctx), 0.0)
        rows.append(jnp.sum(ctx[:heads], axis=0, keepdims=True))
        rows.append(jnp.sum(ctx[heads:], axis=0, keepdims=True))
    return jnp.concatenate(rows + [jnp.zeros((8 - slots, width), f32)], axis=0)


def split_cache(cache, out_ref):
    slots, count, _ = cache.shape
    tiles = out_ref.shape[3] // LANES
    group = 2 * tiles
    step = 256
    part = step // group
    r = lax.broadcasted_iota(jnp.int32, (step, step), 0)
    c = lax.broadcasted_iota(jnp.int32, (step, step), 1)
    order = (c == (r % part) * group + r // part).astype(bf16)
    for slot in range(slots):
        for at in range(count // step):
            rows = dot(order, cache[slot, at * step : (at + 1) * step]).astype(bf16)
            for tile in range(tiles):
                for kind in range(2):
                    g = (tile * 2 + kind) * part
                    out_ref[
                        slot, kind, at * part : (at + 1) * part, tile * LANES : (tile + 1) * LANES
                    ] = rows[g : g + part]
        yield slot


def load_split(source, held, sems, out_ref):
    copies = []
    for slot in range(held.shape[0]):
        copies.append(pltpu.make_async_copy(source.at[slot], held.at[slot], sems.at[slot]))
        copies[-1].start()
    copies[0].wait()
    for slot in split_cache(held, out_ref):
        if slot + 1 < len(copies):
            copies[slot + 1].wait()


def wanted(deal, rows, me, far, back):
    cols = 4 * rows
    row = lax.broadcasted_iota(jnp.int32, (2 * rows, cols), 0)
    col = lax.broadcasted_iota(jnp.int32, (2 * rows, cols), 1)
    take = jnp.where(row < rows, me, me ^ far) * rows + row % rows
    have = (me ^ (col // rows)) * rows + col % rows
    if back:
        for i in range(cols):
            have = jnp.where(col == i, deal[(me ^ (i // rows)) * rows + i % rows], have)
    else:
        for i in range(2 * rows):
            at = (me if i < rows else me ^ far) * rows + i % rows
            take = jnp.where(row == i, deal[at], take)
    return (have == take).astype(bf16)


def plan_kernel(deal, tokens, cache, own_ref, out_ref, back_ref, kv_ref, held, sems, *, far):
    me = lax.axis_index("req")
    rows = tokens.shape[0]
    own_ref[...] = tokens[...]
    out_ref[...] = wanted(deal, rows, me, far, False)
    back_ref[...] = wanted(deal, rows, me, far, True)
    load_split(cache, held, sems, kv_ref)


def split_kernel(cache, kv_ref, held, sems):
    load_split(cache, held, sems, kv_ref)


def sort_kernel(hit, own, g1, g2, g3, mine_ref, theirs_ref):
    rows = own.shape[0]
    whole = jnp.concatenate([p[...] for p in (own, g1, g2, g3)], axis=0)
    out = dot(hit[...], whole)
    mine_ref[...] = out[:rows].astype(bf16)
    theirs_ref[...] = out[rows:].astype(bf16)


def flat(vec):
    return vec[...].astype(f32).reshape(1, vec.shape[0])


def first_kernel(
    lens, mine, more, w_qkv, b_qkv, cache, w_out, x_ref, part_ref, *, heads
):
    slots = x_ref.shape[0]
    x = mine[...].astype(f32) + more[...].astype(f32)
    x_ref[...] = x.astype(bf16)
    x = pad_rows(x, 8).astype(bf16)
    bias = b_qkv[...].astype(f32)
    qkv = [round_rows(dot(x, w_qkv[k]) + bias[k : k + 1]) for k in range(3)]
    length = [lens[s] for s in range(slots)]
    ctx = attend(qkv[0], cache, length, heads, qkv[1], qkv[2])
    part_ref[...] = dot(ctx, w_out[...])[:slots]


def settle(own, p1, p2, p3, x, bias, gain, beta):
    total = own[...] + p1[...] + p2[...] + p3[...] + flat(bias) + x[...].astype(f32)
    return norm_rows(total, flat(gain), flat(beta)).astype(bf16)


def second_kernel(
    lens, own, p1, p2, p3, x, bias, gain, beta, w_cq, b_cq, cache, w_cout, h_ref, part_ref, *, heads
):
    slots = own.shape[0]
    h1 = settle(own, p1, p2, p3, x, bias, gain, beta)
    h_ref[...] = h1
    cq = round_rows(dot(pad_rows(h1.astype(f32), 8), w_cq[...]) + flat(b_cq))
    length = [lens[s] for s in range(slots)]
    ctx = attend(cq, cache, length, heads)
    part_ref[...] = dot(ctx, w_cout[...])[:slots]


def third_kernel(
    own, p1, p2, p3, x, bias, gain, beta, w_up, b_up, w_down, h_ref, part_ref
):
    slots = own.shape[0]
    h2 = settle(own, p1, p2, p3, x, bias, gain, beta)
    h_ref[...] = h2
    hidden = dot(pad_rows(h2.astype(f32), 8), w_up[...]) + flat(b_up)
    act = 0.5 * hidden * (1.0 + lax.erf(hidden * (2.0**-0.5)))
    part_ref[...] = dot(act, w_down[...])[:slots]


def fourth_kernel(own, p1, p2, p3, x, bias, gain, beta, y_ref):
    y_ref[...] = settle(own, p1, p2, p3, x, bias, gain, beta)


def add_kernel(mine, more, out_ref):
    out_ref[...] = (mine[...].astype(f32) + more[...].astype(f32)).astype(bf16)


def call(kernel, out_shapes, args, smem=0, hbm=(), scratch=(), name=None, cost=None):
    vmem = pl.BlockSpec(memory_space=pltpu.VMEM)
    scalar = pl.BlockSpec(memory_space=pltpu.SMEM)
    far = pl.BlockSpec(memory_space=pltpu.HBM)
    outs = [jax.ShapeDtypeStruct(s, d) for s, d in out_shapes]
    specs = [scalar if i < smem else far if i in hbm else vmem for i in range(len(args))]
    if cost is not None:
        cost = pl.CostEstimate(flops=cost, bytes_accessed=0, transcendentals=0)
    return pl.pallas_call(
        kernel,
        out_shape=outs,
        in_specs=specs,
        out_specs=[vmem] * len(outs),
        scratch_shapes=list(scratch),
        compiler_params=pltpu.CompilerParams(vmem_limit_bytes=24 * 2**20),
        cost_estimate=cost,
        name=name,
    )(*args)


def swap(value, axis, size, mask):
    return lax.ppermute(value, axis, [(i, i ^ mask) for i in range(size)])


def pick_rows(onehot, whole):
    return jnp.dot(onehot.astype(whole.dtype), whole, preferred_element_type=f32).astype(whole.dtype)


FAR = 4


def near_swaps(value):
    names, size = ("req", "tp"), lax.axis_size("req") * lax.axis_size("tp")
    tps = lax.axis_size("tp")
    return [swap(value, names, size, mask * tps + 1) for mask in (1, 2, 3)]


def far_swap(value):
    names, size = ("req", "tp"), lax.axis_size("req") * lax.axis_size("tp")
    return swap(value, names, size, FAR * lax.axis_size("tp") + 1)


def sort_rows(hit, own, near, name):
    state = (own.shape, bf16)
    mine, theirs = call(
        sort_kernel, [state, state], [hit, own] + near, name=name, cost=SPARE_FLOPS
    )
    return mine, far_swap(theirs)


def deal_whole(value, deal, back):
    base = lax.axis_index("req") * value.shape[0]
    spread = jnp.arange(value.shape[0], dtype=jnp.int32)
    whole = lax.all_gather(value, "req", axis=0, tiled=True)
    if back:
        onehot = deal[None, :] == (base + spread)[:, None]
    else:
        owner = lax.dynamic_slice_in_dim(deal, base, value.shape[0])
        onehot = owner[:, None] == jnp.arange(deal.shape[0], dtype=jnp.int32)[None, :]
    picked = pick_rows(onehot, whole)
    return picked, jnp.zeros_like(picked)


def split_shapes(cache):
    slots, span, _, width = cache.shape
    tiles = width // LANES
    scratch = [
        pltpu.VMEM((slots, span * 2 * tiles, LANES), bf16),
        pltpu.SemaphoreType.DMA((slots,)),
    ]
    return ((slots, 2, span, width), bf16), scratch


def sum_parts(value, mesh_shape):
    tps = mesh_shape["tp"]
    if tps == 4:
        return [value] + [swap(value, "tp", tps, mask) for mask in (1, 2, 3)]
    whole = lax.psum(value, "tp")
    zero = jnp.zeros_like(whole)
    return [whole, zero, zero, zero]


def on_device(
    mesh_shape,
    tokens,
    deal,
    self_len,
    enc_len,
    self_cache,
    cross_cache,
    w_qkv,
    b_qkv,
    w_out,
    b_out,
    ln1_gain,
    ln1_bias,
    w_cq,
    b_cq,
    w_cout,
    b_cout,
    ln2_gain,
    ln2_bias,
    w_up,
    b_up,
    w_down,
    b_down,
    ln3_gain,
    ln3_bias,
):
    rows, model = tokens.shape
    width = self_cache.shape[3]
    heads = width // HEAD_DIM

    def tile_rows(cache):
        slots, span = cache.shape[0], cache.shape[1]
        split = cache.reshape(slots, span, 2, width // LANES, LANES)
        return split.transpose(0, 1, 3, 2, 4).reshape(slots, -1, LANES)

    state, sums = ((rows, model), bf16), ((rows, model), f32)
    split, scratch = split_shapes(self_cache)
    hops = mesh_shape["req"] == 2 * FAR
    if hops:
        near = near_swaps(tokens)
        hits = ((2 * rows, 4 * rows), bf16)
        own, hit_out, hit_back, self_kv = call(
            functools.partial(plan_kernel, far=FAR),
            [state, hits, hits, split],
            [deal, tokens, tile_rows(self_cache)],
            smem=1,
            hbm=(2,),
            scratch=scratch,
            name="plan",
        )
        mine, more = sort_rows(hit_out, own, near, "sort_out")
    else:
        mine, more = deal_whole(tokens, deal, False)
        (self_kv,) = call(
            split_kernel, [split], [tile_rows(self_cache)], hbm=(0,), scratch=scratch, name="split"
        )
    split, scratch = split_shapes(cross_cache)
    (cross_kv,) = call(
        split_kernel,
        [split],
        [tile_rows(cross_cache)],
        hbm=(0,),
        scratch=scratch,
        name="split_cross",
    )
    x, part = call(
        functools.partial(first_kernel, heads=heads),
        [state, sums],
        [self_len, mine, more, w_qkv.transpose(1, 0, 2), b_qkv, self_kv, w_out],
        smem=1,
        name="self_attention",
    )
    h1, part = call(
        functools.partial(second_kernel, heads=heads),
        [state, sums],
        [enc_len]
        + sum_parts(part, mesh_shape)
        + [x, b_out, ln1_gain, ln1_bias, w_cq, b_cq, cross_kv, w_cout],
        smem=1,
        name="cross_attention",
    )
    h2, part = call(
        third_kernel,
        [state, sums],
        sum_parts(part, mesh_shape)
        + [h1, b_cout, ln2_gain, ln2_bias, w_up, b_up, w_down],
        name="feed_forward",
    )
    (y,) = call(
        fourth_kernel,
        [state],
        sum_parts(part, mesh_shape) + [h2, b_down, ln3_gain, ln3_bias],
        name="last_norm",
    )
    if hops:
        mine, more = sort_rows(hit_back, y, near_swaps(y), "sort_back")
    else:
        mine, more = deal_whole(y, deal, True)
    (result,) = call(add_kernel, [state], [mine, more], name="deal_back")
    return result


def solution(mesh):
    return jax.shard_map(
        functools.partial(on_device, dict(mesh.shape)),
        mesh=mesh,
        in_specs=(
            P("req", None),
            P(),
            P("req"),
            P("req"),
            P("req", None, None, "tp"),
            P("req", None, None, "tp"),
            P(None, None, "tp"),
            P(None, "tp"),
            P("tp", None),
            P(),
            P(),
            P(),
            P(None, "tp"),
            P("tp"),
            P("tp", None),
            P(),
            P(),
            P(),
            P(None, "tp"),
            P("tp"),
            P("tp", None),
            P(),
            P(),
            P(),
        ),
        out_specs=P("req", None),
        check_vma=False,
    )
```

```python
import functools

import jax
import jax.numpy as jnp
from jax import lax
from jax.experimental import pallas as pl
from jax.experimental.pallas import tpu as pltpu
from jax.sharding import PartitionSpec as P

HEAD_DIM = 64
LANES = 128
EPS = 1e-05
MASKED = -1e30
SPARE_FLOPS = 10**10
f32 = jnp.float32
bf16 = jnp.bfloat16


def norm_rows(total, gain, beta):
    mean = jnp.mean(total, axis=-1, keepdims=True)
    centered = total - mean
    var = jnp.mean(centered * centered, axis=-1, keepdims=True)
    return centered / jnp.sqrt(var + EPS) * gain + beta


def round_rows(value):
    return value.astype(bf16).astype(f32)


def dot(a, b):
    return jnp.dot(a.astype(bf16), b, preferred_element_type=f32)


def dot_t(a, b):
    return lax.dot_general(
        a.astype(bf16), b, (((1,), (1,)), ((), ())), preferred_element_type=f32
    )


def pad_rows(value, rows):
    return jnp.concatenate(
        [value, jnp.zeros((rows - value.shape[0], value.shape[1]), value.dtype)], axis=0
    )


def head_rows(vec, slot, heads, first):
    return jnp.where(first, vec[slot : slot + 1], vec[slot + 1 : slot + 2])


def attend(query, cache, lens, heads, fresh_key=None, fresh_value=None):
    where = [(ref, s) for ref in cache for s in range(ref.shape[0])]
    slots = len(where)
    _, _, span, width = cache[0].shape
    pair = 2 * heads
    scale = HEAD_DIM ** (-0.5)
    row = lax.broadcasted_iota(jnp.int32, (pair, width), 0)
    lane = lax.broadcasted_iota(jnp.int32, (pair, width), 1)
    first = row < heads
    own = (lane // HEAD_DIM) == jnp.where(first, row, row - heads)
    first_col = lax.broadcasted_iota(jnp.int32, (pair, span), 0) < heads
    position = lax.broadcasted_iota(jnp.int32, (pair, span), 1)
    rows = []
    for slot in range(0, slots, 2):
        q = jnp.where(own, head_rows(query, slot, heads, first) * scale, 0.0)
        raw = [dot_t(q, ref[at, 0]) for ref, at in where[slot : slot + 2]]
        length = jnp.where(first_col, lens[slot], lens[slot + 1])
        scores = jnp.where(position < length, jnp.where(first_col, raw[0], raw[1]), MASKED)
        top = jnp.max(scores, axis=-1, keepdims=True)
        if fresh_key is not None:
            k_new = head_rows(fresh_key, slot, heads, first)
            v_new = head_rows(fresh_value, slot, heads, first)
            fresh = jnp.sum(q * k_new, axis=-1, keepdims=True)
            top = jnp.maximum(top, fresh)
        expo = jnp.exp(scores - top)
        total = jnp.sum(expo, axis=-1, keepdims=True)
        if fresh_key is not None:
            expn = jnp.exp(fresh - top)
            total = total + expn
        out = [dot(expo, ref[at, 1]) for ref, at in where[slot : slot + 2]]
        ctx = jnp.where(first, out[0], out[1])
        if fresh_key is not None:
            ctx = ctx + round_rows(expn) * v_new
        ctx = jnp.where(own, round_rows(ctx * (1.0 / total)), 0.0)
        rows.append(jnp.sum(ctx[:heads], axis=0, keepdims=True))
        rows.append(jnp.sum(ctx[heads:], axis=0, keepdims=True))
    return jnp.concatenate(rows + [jnp.zeros((8 - slots, width), f32)], axis=0)


def split_cache(cache, out_ref, start):
    slots = out_ref.shape[0]
    count = cache.shape[1]
    tiles = out_ref.shape[3] // LANES
    group = 2 * tiles
    step = 256
    part = step // group
    r = lax.broadcasted_iota(jnp.int32, (step, step), 0)
    c = lax.broadcasted_iota(jnp.int32, (step, step), 1)
    order = (c == (r % part) * group + r // part).astype(bf16)
    for slot in range(slots):
        for at in range(count // step):
            rows = dot(order, cache[start + slot, at * step : (at + 1) * step]).astype(bf16)
            for tile in range(tiles):
                for kind in range(2):
                    g = (tile * 2 + kind) * part
                    out_ref[
                        slot, kind, at * part : (at + 1) * part, tile * LANES : (tile + 1) * LANES
                    ] = rows[g : g + part]


def wanted(deal, rows, me, far, back):
    cols = 4 * rows
    row = lax.broadcasted_iota(jnp.int32, (2 * rows, cols), 0)
    col = lax.broadcasted_iota(jnp.int32, (2 * rows, cols), 1)
    take = jnp.where(row < rows, me, me ^ far) * rows + row % rows
    have = (me ^ (col // rows)) * rows + col % rows
    if back:
        for i in range(cols):
            have = jnp.where(col == i, deal[(me ^ (i // rows)) * rows + i % rows], have)
    else:
        for i in range(2 * rows):
            at = (me if i < rows else me ^ far) * rows + i % rows
            take = jnp.where(row == i, deal[at], take)
    return (have == take).astype(bf16)


def stub_kernel(out_ref):
    out_ref[...] = jnp.zeros_like(out_ref)


def plan_kernel(deal, stub, tokens, cache, own_ref, out_ref, back_ref, kv_ref, *, far):
    me = lax.axis_index("req")
    rows = tokens.shape[0]
    own_ref[...] = tokens[...]
    out_ref[...] = wanted(deal, rows, me, far, False)
    back_ref[...] = wanted(deal, rows, me, far, True)
    split_cache(cache, kv_ref, 0)


def split_kernel(after, cache, kv_ref, *, start):
    split_cache(cache, kv_ref, start)


def sort_kernel(hit, own, g1, g2, g3, mine_ref, theirs_ref):
    rows = own.shape[0]
    whole = jnp.concatenate([p[...] for p in (own, g1, g2, g3)], axis=0)
    out = dot(hit[...], whole)
    mine_ref[...] = out[:rows].astype(bf16)
    theirs_ref[...] = out[rows:].astype(bf16)


def flat(vec):
    return vec[...].astype(f32).reshape(1, vec.shape[0])


def first_kernel(
    lens, mine, more, w_qkv, b_qkv, w_out, *refs, heads
):
    *cache, x_ref, part_ref = refs
    slots = x_ref.shape[0]
    x = mine[...].astype(f32) + more[...].astype(f32)
    x_ref[...] = x.astype(bf16)
    x = pad_rows(x, 8).astype(bf16)
    bias = b_qkv[...].astype(f32)
    qkv = [round_rows(dot(x, w_qkv[k]) + bias[k : k + 1]) for k in range(3)]
    length = [lens[s] for s in range(slots)]
    ctx = attend(qkv[0], cache, length, heads, qkv[1], qkv[2])
    part_ref[...] = dot(ctx, w_out[...])[:slots]


def settle(own, p1, p2, p3, x, bias, gain, beta):
    total = own[...] + p1[...] + p2[...] + p3[...] + flat(bias) + x[...].astype(f32)
    return norm_rows(total, flat(gain), flat(beta)).astype(bf16)


def second_kernel(
    lens, own, p1, p2, p3, x, bias, gain, beta, w_cq, b_cq, cache, w_cout, h_ref, part_ref, *, heads
):
    slots = own.shape[0]
    h1 = settle(own, p1, p2, p3, x, bias, gain, beta)
    h_ref[...] = h1
    cq = round_rows(dot(pad_rows(h1.astype(f32), 8), w_cq[...]) + flat(b_cq))
    length = [lens[s] for s in range(slots)]
    ctx = attend(cq, [cache], length, heads)
    part_ref[...] = dot(ctx, w_cout[...])[:slots]


def third_kernel(
    own, p1, p2, p3, x, bias, gain, beta, w_up, b_up, w_down, h_ref, part_ref
):
    slots = own.shape[0]
    h2 = settle(own, p1, p2, p3, x, bias, gain, beta)
    h_ref[...] = h2
    hidden = dot(pad_rows(h2.astype(f32), 8), w_up[...]) + flat(b_up)
    act = 0.5 * hidden * (1.0 + lax.erf(hidden * (2.0**-0.5)))
    part_ref[...] = dot(act, w_down[...])[:slots]


def fourth_kernel(own, p1, p2, p3, x, bias, gain, beta, y_ref):
    y_ref[...] = settle(own, p1, p2, p3, x, bias, gain, beta)


def add_kernel(mine, more, out_ref):
    out_ref[...] = (mine[...].astype(f32) + more[...].astype(f32)).astype(bf16)


def call(kernel, out_shapes, args, smem=0, name=None, cost=None):
    vmem = pl.BlockSpec(memory_space=pltpu.VMEM)
    scalar = pl.BlockSpec(memory_space=pltpu.SMEM)
    outs = [jax.ShapeDtypeStruct(s, d) for s, d in out_shapes]
    specs = [scalar if i < smem else vmem for i in range(len(args))]
    if cost is not None:
        cost = pl.CostEstimate(flops=cost, bytes_accessed=0, transcendentals=0)
    made = pl.pallas_call(
        kernel,
        out_shape=outs,
        in_specs=specs,
        out_specs=[vmem] * len(outs),
        compiler_params=pltpu.CompilerParams(vmem_limit_bytes=24 * 2**20),
        cost_estimate=cost,
        name=name,
    )(*args)
    return list(made)


def swap(value, axis, size, mask):
    return lax.ppermute(value, axis, [(i, i ^ mask) for i in range(size)])


def pick_rows(onehot, whole):
    return jnp.dot(onehot.astype(whole.dtype), whole, preferred_element_type=f32).astype(whole.dtype)


FAR = 4


def near_swaps(value):
    names, size = ("req", "tp"), lax.axis_size("req") * lax.axis_size("tp")
    tps = lax.axis_size("tp")
    return [swap(value, names, size, mask * tps + 1) for mask in (1, 2, 3)]


def far_swap(value):
    names, size = ("req", "tp"), lax.axis_size("req") * lax.axis_size("tp")
    return swap(value, names, size, FAR * lax.axis_size("tp") + 1)


def sort_rows(hit, own, near, name):
    state = (own.shape, bf16)
    mine, theirs = call(
        sort_kernel, [state, state], [hit, own] + near, name=name, cost=SPARE_FLOPS
    )
    return mine, far_swap(theirs)


def deal_whole(value, deal, back):
    base = lax.axis_index("req") * value.shape[0]
    spread = jnp.arange(value.shape[0], dtype=jnp.int32)
    whole = lax.all_gather(value, "req", axis=0, tiled=True)
    if back:
        onehot = deal[None, :] == (base + spread)[:, None]
    else:
        owner = lax.dynamic_slice_in_dim(deal, base, value.shape[0])
        onehot = owner[:, None] == jnp.arange(deal.shape[0], dtype=jnp.int32)[None, :]
    picked = pick_rows(onehot, whole)
    return picked, jnp.zeros_like(picked)


def split_part(after, cache, start, slots, name):
    _, span, _, width = cache.shape
    return call(
        functools.partial(split_kernel, start=start),
        [((slots, 2, span, width), bf16)],
        [after, tile_rows(cache)],
        name=name,
    )


def tile_rows(cache):
    slots, span, _, width = cache.shape
    split = cache.reshape(slots, span, 2, width // LANES, LANES)
    return split.transpose(0, 1, 3, 2, 4).reshape(slots, -1, LANES)


def sum_parts(value, mesh_shape):
    tps = mesh_shape["tp"]
    if tps == 4:
        return [value] + [swap(value, "tp", tps, mask) for mask in (1, 2, 3)]
    whole = lax.psum(value, "tp")
    zero = jnp.zeros_like(whole)
    return [whole, zero, zero, zero]


def on_device(
    mesh_shape,
    tokens,
    deal,
    self_len,
    enc_len,
    self_cache,
    cross_cache,
    w_qkv,
    b_qkv,
    w_out,
    b_out,
    ln1_gain,
    ln1_bias,
    w_cq,
    b_cq,
    w_cout,
    b_cout,
    ln2_gain,
    ln2_bias,
    w_up,
    b_up,
    w_down,
    b_down,
    ln3_gain,
    ln3_bias,
):
    rows, model = tokens.shape
    width = self_cache.shape[3]
    heads = width // HEAD_DIM

    state, sums = ((rows, model), bf16), ((rows, model), f32)
    hops = mesh_shape["req"] == 2 * FAR
    if hops:
        near = near_swaps(tokens)
        hits = ((2 * rows, 4 * rows), bf16)
        half = rows // 2
        (stub,) = call(stub_kernel, [((8, LANES), f32)], [], name="stub", cost=SPARE_FLOPS)
        own, hit_out, hit_back, kv = call(
            functools.partial(plan_kernel, far=FAR),
            [state, hits, hits, ((half, 2, self_cache.shape[1], width), bf16)],
            [deal, stub, tokens, tile_rows(self_cache)],
            smem=1,
            name="plan",
        )
        mine, more = sort_rows(hit_out, own, near, "sort_out")
        self_kv = [kv] + split_part(mine, self_cache, half, rows - half, "split_self")
    else:
        mine, more = deal_whole(tokens, deal, False)
        self_kv = split_part(mine, self_cache, 0, rows, "split_self")
    x, part = call(
        functools.partial(first_kernel, heads=heads),
        [state, sums],
        [self_len, mine, more, w_qkv.transpose(1, 0, 2), b_qkv, w_out] + list(self_kv),
        smem=1,
        name="self_attention",
    )
    (cross_kv,) = split_part(x, cross_cache, 0, rows, "split_cross")
    h1, part = call(
        functools.partial(second_kernel, heads=heads),
        [state, sums],
        [enc_len]
        + sum_parts(part, mesh_shape)
        + [x, b_out, ln1_gain, ln1_bias, w_cq, b_cq, cross_kv, w_cout],
        smem=1,
        name="cross_attention",
    )
    h2, part = call(
        third_kernel,
        [state, sums],
        sum_parts(part, mesh_shape)
        + [h1, b_cout, ln2_gain, ln2_bias, w_up, b_up, w_down],
        name="feed_forward",
    )
    (y,) = call(
        fourth_kernel,
        [state],
        sum_parts(part, mesh_shape) + [h2, b_down, ln3_gain, ln3_bias],
        name="last_norm",
    )
    if hops:
        mine, more = sort_rows(hit_back, y, near_swaps(y), "sort_back")
    else:
        mine, more = deal_whole(y, deal, True)
    (result,) = call(add_kernel, [state], [mine, more], name="deal_back")
    return result


def solution(mesh):
    return jax.shard_map(
        functools.partial(on_device, dict(mesh.shape)),
        mesh=mesh,
        in_specs=(
            P("req", None),
            P(),
            P("req"),
            P("req"),
            P("req", None, None, "tp"),
            P("req", None, None, "tp"),
            P(None, None, "tp"),
            P(None, "tp"),
            P("tp", None),
            P(),
            P(),
            P(),
            P(None, "tp"),
            P("tp"),
            P("tp", None),
            P(),
            P(),
            P(),
            P(None, "tp"),
            P("tp"),
            P("tp", None),
            P(),
            P(),
            P(),
        ),
        out_specs=P("req", None),
        check_vma=False,
    )
```

```python
import functools

import jax
import jax.numpy as jnp
from jax import lax
from jax.experimental import pallas as pl
from jax.experimental.pallas import tpu as pltpu
from jax.sharding import PartitionSpec as P

HEAD_DIM = 64
LANES = 128
EPS = 1e-05
MASKED = -1e30
SPARE_FLOPS = 10**10
NORM_1, NORM_2, NORM_3, B_UP, B_CQ, B_QKV, TABLE_ROWS = 0, 3, 6, 9, 10, 11, 16
f32 = jnp.float32
bf16 = jnp.bfloat16


def norm_rows(total, gain, beta):
    mean = jnp.mean(total, axis=-1, keepdims=True)
    centered = total - mean
    var = jnp.mean(centered * centered, axis=-1, keepdims=True)
    return centered / jnp.sqrt(var + EPS) * gain + beta


def round_rows(value):
    return value.astype(bf16).astype(f32)


def dot(a, b):
    return jnp.dot(a.astype(bf16), b, preferred_element_type=f32)


def dot_t(a, b):
    return lax.dot_general(
        a.astype(bf16), b, (((1,), (1,)), ((), ())), preferred_element_type=f32
    )


def pad_rows(value, rows):
    return jnp.concatenate(
        [value, jnp.zeros((rows - value.shape[0], value.shape[1]), value.dtype)], axis=0
    )


def head_rows(vec, slot, heads, first):
    return jnp.where(first, vec[slot : slot + 1], vec[slot + 1 : slot + 2])


def attend(query, cache, limits, heads, fresh_key=None, fresh_value=None):
    where = [(ref, s) for ref in cache for s in range(ref.shape[0])]
    slots = len(where)
    _, _, span, width = cache[0].shape
    pair = 2 * heads
    scale = HEAD_DIM ** (-0.5)
    row = lax.broadcasted_iota(jnp.int32, (pair, width), 0)
    lane = lax.broadcasted_iota(jnp.int32, (pair, width), 1)
    first = row < heads
    own = (lane // HEAD_DIM) == jnp.where(first, row, row - heads)
    first_col = lax.broadcasted_iota(jnp.int32, (pair, span), 0) < heads
    position = lax.broadcasted_iota(jnp.int32, (pair, span), 1)
    rows = []
    for slot in range(0, slots, 2):
        q = jnp.where(own, head_rows(query, slot, heads, first) * scale, 0.0)
        raw = [dot_t(q, ref[at, 0]) for ref, at in where[slot : slot + 2]]
        length = limits[slot * heads : (slot + 2) * heads]
        length = jnp.concatenate([length] * (span // LANES), axis=1)
        scores = jnp.where(position < length, jnp.where(first_col, raw[0], raw[1]), MASKED)
        top = jnp.max(scores, axis=-1, keepdims=True)
        if fresh_key is not None:
            k_new = head_rows(fresh_key, slot, heads, first)
            v_new = head_rows(fresh_value, slot, heads, first)
            fresh = jnp.sum(q * k_new, axis=-1, keepdims=True)
            top = jnp.maximum(top, fresh)
        expo = jnp.exp(scores - top)
        total = jnp.sum(expo, axis=-1, keepdims=True)
        if fresh_key is not None:
            expn = jnp.exp(fresh - top)
            total = total + expn
        out = [dot(expo, ref[at, 1]) for ref, at in where[slot : slot + 2]]
        ctx = jnp.where(first, out[0], out[1])
        if fresh_key is not None:
            ctx = ctx + round_rows(expn) * v_new
        ctx = jnp.where(own, round_rows(ctx * (1.0 / total)), 0.0)
        rows.append(jnp.sum(ctx[:heads], axis=0, keepdims=True))
        rows.append(jnp.sum(ctx[heads:], axis=0, keepdims=True))
    return jnp.concatenate(rows + [jnp.zeros((8 - slots, width), f32)], axis=0)


def split_cache(cache, out_ref, start):
    slots = out_ref.shape[0]
    count = cache.shape[1]
    tiles = out_ref.shape[3] // LANES
    group = 2 * tiles
    step = 256
    part = step // group
    r = lax.broadcasted_iota(jnp.int32, (step, step), 0)
    c = lax.broadcasted_iota(jnp.int32, (step, step), 1)
    order = (c == (r % part) * group + r // part).astype(bf16)
    for slot in range(slots):
        for at in range(count // step):
            rows = dot(order, cache[start + slot, at * step : (at + 1) * step]).astype(bf16)
            for tile in range(tiles):
                for kind in range(2):
                    g = (tile * 2 + kind) * part
                    out_ref[
                        slot, kind, at * part : (at + 1) * part, tile * LANES : (tile + 1) * LANES
                    ] = rows[g : g + part]


def wanted(deal, rows, me, core, back):
    blocks = len(GATHER[0])
    shape = (8, blocks * rows)
    row = lax.broadcasted_iota(jnp.int32, shape, 0)
    col = lax.broadcasted_iota(jnp.int32, shape, 1)
    origin = [me ^ jnp.where(core == 0, a, max(b, 0)) for a, b in zip(*GATHER)]
    used = [(core == 0) | (b >= 0) for b in GATHER[1]]
    take, have = me * rows + row, jnp.full(shape, -1, jnp.int32)
    for i in range(blocks * rows):
        ident = origin[i // rows] * rows + i % rows
        ident = jnp.where(used[i // rows], deal[ident] if back else ident, -1)
        have = jnp.where(col == i, ident, have)
    if not back:
        for i in range(rows):
            take = jnp.where(row == i, deal[me * rows + i], take)
    return ((have == take) & (row < rows)).astype(bf16)


def stub_kernel(out_ref):
    out_ref[...] = jnp.zeros_like(out_ref)


def spread_lengths(lens, ref, heads):
    slot = lax.broadcasted_iota(jnp.int32, ref.shape, 0) // heads
    out = jnp.zeros(ref.shape, jnp.int32)
    for s in range(ref.shape[0] // heads):
        out = jnp.where(slot == s, lens[s], out)
    ref[...] = out


def table_kernel(*refs):
    *vecs, table_ref = refs
    table_ref[...] = jnp.zeros_like(table_ref)
    for i, vec in enumerate(vecs):
        if len(vec.shape) == 1:
            table_ref[i : i + 1, : vec.shape[0]] = vec[...].astype(f32).reshape(1, vec.shape[0])
        else:
            table_ref[i : i + vec.shape[0], : vec.shape[1]] = vec[...].astype(f32)


def plan_kernel(deal, self_len, enc_len, stub, tokens, cache, *refs, heads):
    *vecs, own_ref, out_ref, back_ref, self_ref, enc_ref, kv_ref, table_ref = refs
    table_kernel(*vecs, table_ref)
    spread_lengths(self_len, self_ref, heads)
    spread_lengths(enc_len, enc_ref, heads)
    me, core = lax.axis_index("req"), lax.axis_index("tp") % 2
    rows = tokens.shape[0]
    own_ref[...] = tokens[...]
    out_ref[...] = wanted(deal, rows, me, core, False)
    back_ref[...] = wanted(deal, rows, me, core, True)
    split_cache(cache, kv_ref, 0)


def split_kernel(after, cache, kv_ref, *, start):
    split_cache(cache, kv_ref, start)


def sort_kernel(hit, *refs):
    *blocks, out_ref = refs
    whole = jnp.concatenate([p[...] for p in blocks], axis=0)
    out_ref[...] = dot(hit[...], whole)[: out_ref.shape[0]].astype(bf16)


def first_kernel(
    limits, mine, more, w_qkv, vecs, w_out, *refs, heads
):
    *cache, x_ref, part_ref = refs
    slots = x_ref.shape[0]
    x = mine[...].astype(f32) + more[...].astype(f32)
    x_ref[...] = x.astype(bf16)
    x = pad_rows(x, 8).astype(bf16)
    width = w_out.shape[0]
    bias = [vecs[B_QKV + k : B_QKV + k + 1, :width] for k in range(3)]
    qkv = [round_rows(dot(x, w_qkv[k]) + bias[k]) for k in range(3)]
    ctx = attend(qkv[0], cache, limits, heads, qkv[1], qkv[2])
    part_ref[...] = dot(ctx, w_out[...])[:slots].astype(bf16)


def settle(parts, x, vecs, at):
    total = vecs[at : at + 1] + x[...].astype(f32)
    for part in parts:
        total = total + part[...].astype(f32)
    return norm_rows(total, vecs[at + 1 : at + 2], vecs[at + 2 : at + 3]).astype(bf16)


def second_kernel(limits, p0, p1, p2, p3, x, vecs, w_cq, cache, w_cout, h_ref, part_ref, *, heads):
    slots = p0.shape[0]
    h1 = settle((p0, p1, p2, p3), x, vecs, NORM_1)
    h_ref[...] = h1
    bias = vecs[B_CQ : B_CQ + 1, : w_cq.shape[1]]
    cq = round_rows(dot(pad_rows(h1.astype(f32), 8), w_cq[...]) + bias)
    ctx = attend(cq, [cache], limits, heads)
    part_ref[...] = dot(ctx, w_cout[...])[:slots].astype(bf16)


def third_kernel(p0, p1, p2, p3, x, vecs, w_up, w_down, h_ref, part_ref):
    slots = p0.shape[0]
    h2 = settle((p0, p1, p2, p3), x, vecs, NORM_2)
    h_ref[...] = h2
    bias = vecs[B_UP : B_UP + 1, : w_up.shape[1]]
    hidden = dot(pad_rows(h2.astype(f32), 8), w_up[...]) + bias
    act = 0.5 * hidden * (1.0 + lax.erf(hidden * (2.0**-0.5)))
    part_ref[...] = dot(act, w_down[...])[:slots].astype(bf16)


def fourth_kernel(p0, p1, p2, p3, x, vecs, y_ref):
    y_ref[...] = settle((p0, p1, p2, p3), x, vecs, NORM_3)


def add_kernel(mine, more, out_ref):
    out_ref[...] = (mine[...].astype(f32) + more[...].astype(f32)).astype(bf16)


def call(kernel, out_shapes, args, smem=0, name=None, cost=None):
    vmem = pl.BlockSpec(memory_space=pltpu.VMEM)
    scalar = pl.BlockSpec(memory_space=pltpu.SMEM)
    outs = [jax.ShapeDtypeStruct(s, d) for s, d in out_shapes]
    specs = [scalar if i < smem else vmem for i in range(len(args))]
    if cost is not None:
        cost = pl.CostEstimate(flops=cost, bytes_accessed=0, transcendentals=0)
    made = pl.pallas_call(
        kernel,
        out_shape=outs,
        in_specs=specs,
        out_specs=[vmem] * len(outs),
        compiler_params=pltpu.CompilerParams(vmem_limit_bytes=24 * 2**20),
        cost_estimate=cost,
        name=name,
    )(*args)
    return list(made)


def swap(value, axis, size, mask):
    return lax.ppermute(value, axis, [(i, i ^ mask) for i in range(size)])


def pick_rows(onehot, whole):
    return jnp.dot(onehot.astype(whole.dtype), whole, preferred_element_type=f32).astype(whole.dtype)


GATHER = ((0, 1, 3, 6, 7), (-1, -1, 2, 4, 5))


def in_order(swaps):
    return list(lax.optimization_barrier(swaps))


def gather_blocks(value, mesh_shape, far_first):
    reqs, tps = mesh_shape["req"], mesh_shape["tp"]
    masks = list(zip(*GATHER))[1:]
    got = []
    for a, b in masks if far_first else masks[::-1]:
        b = a if b < 0 else b
        pairs = []
        for r in range(reqs):
            for t in range(tps):
                pairs.append(((r ^ (b if t % 2 else a)) * tps + (t ^ 1), r * tps + t))
        got.append(lax.ppermute(value, ("req", "tp"), pairs))
    got = in_order(got)
    return got if far_first else got[::-1]


def sort_rows(hit, own, got, mesh_shape, name):
    (mine,) = call(
        sort_kernel, [(own.shape, bf16)], [hit, own] + got, name=name
    )
    return mine, swap(mine, "tp", mesh_shape["tp"], 1)


def deal_whole(value, deal, back):
    base = lax.axis_index("req") * value.shape[0]
    spread = jnp.arange(value.shape[0], dtype=jnp.int32)
    whole = lax.all_gather(value, "req", axis=0, tiled=True)
    if back:
        onehot = deal[None, :] == (base + spread)[:, None]
    else:
        owner = lax.dynamic_slice_in_dim(deal, base, value.shape[0])
        onehot = owner[:, None] == jnp.arange(deal.shape[0], dtype=jnp.int32)[None, :]
    picked = pick_rows(onehot, whole)
    return picked, jnp.zeros_like(picked)


def split_part(after, cache, start, slots, name):
    _, span, _, width = cache.shape
    return call(
        functools.partial(split_kernel, start=start),
        [((slots, 2, span, width), bf16)],
        [after, tile_rows(cache)],
        name=name,
    )


def tile_rows(cache):
    slots, span, _, width = cache.shape
    split = cache.reshape(slots, span, 2, width // LANES, LANES)
    return split.transpose(0, 1, 3, 2, 4).reshape(slots, -1, LANES)


def sum_parts(value, mesh_shape):
    tps = mesh_shape["tp"]
    if tps == 4:
        return [value] + in_order([swap(value, "tp", tps, mask) for mask in (1, 2, 3)])
    whole = lax.psum(value.astype(f32), "tp")
    zero = jnp.zeros_like(whole)
    return [whole, zero, zero, zero]


def on_device(
    mesh_shape,
    tokens,
    deal,
    self_len,
    enc_len,
    self_cache,
    cross_cache,
    w_qkv,
    b_qkv,
    w_out,
    b_out,
    ln1_gain,
    ln1_bias,
    w_cq,
    b_cq,
    w_cout,
    b_cout,
    ln2_gain,
    ln2_bias,
    w_up,
    b_up,
    w_down,
    b_down,
    ln3_gain,
    ln3_bias,
):
    rows, model = tokens.shape
    width = self_cache.shape[3]
    heads = width // HEAD_DIM

    state, sums = ((rows, model), bf16), ((rows, model), bf16)
    vecs = [b_out, ln1_gain, ln1_bias, b_cout, ln2_gain, ln2_bias, b_down, ln3_gain, ln3_bias]
    vecs += [b_up, b_cq, b_qkv]
    table = ((TABLE_ROWS, max(model, b_up.shape[0])), f32)
    hops = mesh_shape["req"] == 8 and mesh_shape["tp"] == 4
    if hops:
        got = gather_blocks(tokens, mesh_shape, False)
        hits = ((8, len(GATHER[0]) * rows), bf16)
        half = rows // 2
        (stub,) = call(stub_kernel, [((8, LANES), f32)], [], name="stub", cost=SPARE_FLOPS)
        limits = ((rows * heads, LANES), jnp.int32)
        own, hit_out, hit_back, self_limits, enc_limits, kv, vecs = call(
            functools.partial(plan_kernel, heads=heads),
            [state, hits, hits, limits, limits, ((half, 2, self_cache.shape[1], width), bf16), table],
            [deal, self_len, enc_len, stub, tokens, tile_rows(self_cache)] + vecs,
            smem=3,
            name="plan",
        )
        mine, more = sort_rows(hit_out, own, got, mesh_shape, "sort_out")
        self_kv = [kv] + split_part(mine, self_cache, half, rows - half, "split_self")
    else:
        mine, more = deal_whole(tokens, deal, False)
        (vecs,) = call(table_kernel, [table], vecs, name="table")
        self_limits, enc_limits = (
            jnp.broadcast_to(jnp.repeat(lens, heads)[:, None], (rows * heads, LANES))
            for lens in (self_len, enc_len)
        )
        self_kv = split_part(mine, self_cache, 0, rows, "split_self")
    x, part = call(
        functools.partial(first_kernel, heads=heads),
        [state, sums],
        [self_limits, mine, more, w_qkv.transpose(1, 0, 2), vecs, w_out] + self_kv,
        name="self_attention",
    )
    (cross_kv,) = split_part(x, cross_cache, 0, rows, "split_cross")
    h1, part = call(
        functools.partial(second_kernel, heads=heads),
        [state, sums],
        [enc_limits]
        + sum_parts(part, mesh_shape)
        + [x, vecs, w_cq, cross_kv, w_cout],
        name="cross_attention",
    )
    h2, part = call(
        third_kernel,
        [state, sums],
        sum_parts(part, mesh_shape) + [h1, vecs, w_up, w_down],
        name="feed_forward",
    )
    (y,) = call(
        fourth_kernel,
        [state],
        sum_parts(part, mesh_shape) + [h2, vecs],
        name="last_norm",
    )
    if hops:
        got = gather_blocks(y, mesh_shape, True)
        mine, more = sort_rows(hit_back, y, got, mesh_shape, "sort_back")
    else:
        mine, more = deal_whole(y, deal, True)
    (result,) = call(add_kernel, [state], [mine, more], name="deal_back")
    return result


def solution(mesh):
    return jax.shard_map(
        functools.partial(on_device, dict(mesh.shape)),
        mesh=mesh,
        in_specs=(
            P("req", None),
            P(),
            P("req"),
            P("req"),
            P("req", None, None, "tp"),
            P("req", None, None, "tp"),
            P(None, None, "tp"),
            P(None, "tp"),
            P("tp", None),
            P(),
            P(),
            P(),
            P(None, "tp"),
            P("tp"),
            P("tp", None),
            P(),
            P(),
            P(),
            P(None, "tp"),
            P("tp"),
            P("tp", None),
            P(),
            P(),
            P(),
        ),
        out_specs=P("req", None),
        check_vma=False,
    )
```

```python
import functools

import jax
import jax.numpy as jnp
from jax import lax
from jax.experimental import pallas as pl
from jax.experimental.pallas import tpu as pltpu
from jax.sharding import PartitionSpec as P

HEAD_DIM = 64
LANES = 128
EPS = 1e-05
MASKED = -1e30
SPARE_FLOPS = 10**10
OUT_STEPS = ((7, 5, 1), (6, 4, 1), (1, 1, 1), (2, 3, 1))
BACK_STEPS = ((1, 1, 1), (2, 3, 1), (6, 4, 1), (5, 7, 1))
TP_STEPS = (1, 2, 3)
NORM_1, NORM_2, NORM_3, B_UP, B_CQ, B_QKV, TABLE_ROWS = 0, 3, 6, 9, 10, 11, 16
f32 = jnp.float32
bf16 = jnp.bfloat16


def norm_rows(total, gain, beta):
    mean = jnp.mean(total, axis=-1, keepdims=True)
    centered = total - mean
    var = jnp.mean(centered * centered, axis=-1, keepdims=True)
    return centered / jnp.sqrt(var + EPS) * gain + beta


def round_rows(value):
    return value.astype(bf16).astype(f32)


def dot(a, b):
    return jnp.dot(a.astype(bf16), b, preferred_element_type=f32)


def pad_rows(value, rows):
    return jnp.concatenate(
        [value, jnp.zeros((rows - value.shape[0], value.shape[1]), value.dtype)], axis=0
    )


def head_rows(vec, slot, heads, first):
    return jnp.where(first, vec[slot : slot + 1], vec[slot + 1 : slot + 2])


def attend(query, cache, limits, heads, fresh_key=None, fresh_value=None):
    where = [(k.at[s], v.at[s]) for k, v in cache for s in range(k.shape[0])]
    slots = len(where)
    _, span, width = cache[0][1].shape
    pair = 2 * heads
    scale = HEAD_DIM ** (-0.5)
    row = lax.broadcasted_iota(jnp.int32, (pair, width), 0)
    lane = lax.broadcasted_iota(jnp.int32, (pair, width), 1)
    first = row < heads
    own = (lane // HEAD_DIM) == jnp.where(first, row, row - heads)
    first_col = lax.broadcasted_iota(jnp.int32, (pair, span), 0) < heads
    position = lax.broadcasted_iota(jnp.int32, (pair, span), 1)
    rows = []
    for slot in range(0, slots, 2):
        q = jnp.where(own, head_rows(query, slot, heads, first) * scale, 0.0)
        raw = [dot(q, keys[...]) for keys, _ in where[slot : slot + 2]]
        length = limits[slot * heads : (slot + 2) * heads]
        length = jnp.concatenate([length] * (span // LANES), axis=1)
        scores = jnp.where(position < length, jnp.where(first_col, raw[0], raw[1]), MASKED)
        top = jnp.max(scores, axis=-1, keepdims=True)
        if fresh_key is not None:
            k_new = head_rows(fresh_key, slot, heads, first)
            v_new = head_rows(fresh_value, slot, heads, first)
            fresh = jnp.sum(q * k_new, axis=-1, keepdims=True)
            top = jnp.maximum(top, fresh)
        expo = jnp.exp(scores - top)
        total = jnp.sum(expo, axis=-1, keepdims=True)
        if fresh_key is not None:
            expn = jnp.exp(fresh - top)
            total = total + expn
        out = [dot(expo, values[...]) for _, values in where[slot : slot + 2]]
        ctx = jnp.where(first, out[0], out[1])
        if fresh_key is not None:
            ctx = ctx + round_rows(expn) * v_new
        ctx = jnp.where(own, round_rows(ctx * (1.0 / total)), 0.0)
        rows.append(jnp.sum(ctx[:heads], axis=0, keepdims=True))
        rows.append(jnp.sum(ctx[heads:], axis=0, keepdims=True))
    return jnp.concatenate(rows + [jnp.zeros((8 - slots, width), f32)], axis=0)


def split_cache(cache, key_ref, value_ref, start):
    slots, _, width = value_ref.shape
    count = cache.shape[1]
    tiles = width // LANES
    group = 2 * tiles
    step = 256
    part = step // group
    r = lax.broadcasted_iota(jnp.int32, (step, step), 0)
    c = lax.broadcasted_iota(jnp.int32, (step, step), 1)
    order = (c == (r % part) * group + r // part).astype(bf16)
    pieces = LANES // part
    for slot in range(slots):
        for at in range(0, count // step, pieces):
            rows = [
                dot(order, cache[start + slot, (at + i) * step : (at + i + 1) * step])
                for i in range(pieces)
            ]
            here = slice(at * part, (at + pieces) * part)
            for tile in range(tiles):
                lanes = slice(tile * LANES, (tile + 1) * LANES)
                g = 2 * tile * part
                key = jnp.concatenate([x[g : g + part] for x in rows], axis=0)
                value = jnp.concatenate([x[g + part : g + 2 * part] for x in rows], axis=0)
                key_ref[slot, lanes, here] = key.T.astype(bf16)
                value_ref[slot, here, lanes] = value.astype(bf16)


def wanted(deal, rows, me, core, steps, back):
    masks, seen = [(0, 0, 0)] + list(steps), set()
    origin, used = [], []
    for a, b, _ in masks:
        origin.append(me ^ jnp.where(core == 0, a, b))
        fresh = (a not in seen, b not in seen | {a})
        seen |= {a, b}
        used.append(jnp.where(core == 0, fresh[0], fresh[1]))
    shape = (8, len(masks) * rows)
    row = lax.broadcasted_iota(jnp.int32, shape, 0)
    col = lax.broadcasted_iota(jnp.int32, shape, 1)
    take, have = me * rows + row, jnp.full(shape, -1, jnp.int32)
    for i in range(shape[1]):
        ident = origin[i // rows] * rows + i % rows
        ident = jnp.where(used[i // rows], deal[ident] if back else ident, -1)
        have = jnp.where(col == i, ident, have)
    if not back:
        for i in range(rows):
            take = jnp.where(row == i, deal[me * rows + i], take)
    return ((have == take) & (row < rows)).astype(bf16)


def stub_kernel(out_ref):
    out_ref[...] = jnp.zeros_like(out_ref)


def spread_lengths(lens, ref, heads):
    slot = lax.broadcasted_iota(jnp.int32, ref.shape, 0) // heads
    out = jnp.zeros(ref.shape, jnp.int32)
    for s in range(ref.shape[0] // heads):
        out = jnp.where(slot == s, lens[s], out)
    ref[...] = out


def table_kernel(*refs):
    *vecs, table_ref = refs
    table_ref[...] = jnp.zeros_like(table_ref)
    for i, vec in enumerate(vecs):
        if len(vec.shape) == 1:
            table_ref[i : i + 1, : vec.shape[0]] = vec[...].astype(f32).reshape(1, vec.shape[0])
        else:
            table_ref[i : i + vec.shape[0], : vec.shape[1]] = vec[...].astype(f32)


def plan_kernel(deal, self_len, enc_len, stub, tokens, cache, *refs, heads):
    *vecs, own_ref, out_ref, back_ref, self_ref, enc_ref, key_ref, value_ref, table_ref = refs
    table_kernel(*vecs, table_ref)
    spread_lengths(self_len, self_ref, heads)
    spread_lengths(enc_len, enc_ref, heads)
    me, core = lax.axis_index("req"), lax.axis_index("tp") % 2
    rows = tokens.shape[0]
    own_ref[...] = tokens[...]
    out_ref[...] = wanted(deal, rows, me, core, OUT_STEPS, False)
    back_ref[...] = wanted(deal, rows, me, core, BACK_STEPS, True)
    split_cache(cache, key_ref, value_ref, 0)


def split_kernel(after, cache, key_ref, value_ref, *, start):
    split_cache(cache, key_ref, value_ref, start)


def sort_kernel(hit, *refs):
    *blocks, out_ref = refs
    whole = jnp.concatenate([p[...] for p in blocks], axis=0)
    out_ref[...] = dot(hit[...], whole)[: out_ref.shape[0]].astype(bf16)


def first_kernel(
    limits, mine, more, w_qkv, vecs, w_out, *refs, heads
):
    *cache, x_ref, part_ref = refs
    cache = list(zip(cache[::2], cache[1::2]))
    slots = x_ref.shape[0]
    x = mine[...].astype(f32) + more[...].astype(f32)
    x_ref[...] = x.astype(bf16)
    x = pad_rows(x, 8).astype(bf16)
    width = w_out.shape[0]
    bias = [vecs[B_QKV + k : B_QKV + k + 1, :width] for k in range(3)]
    qkv = [round_rows(dot(x, w_qkv[k]) + bias[k]) for k in range(3)]
    ctx = attend(qkv[0], cache, limits, heads, qkv[1], qkv[2])
    part_ref[...] = dot(ctx, w_out[...])[:slots].astype(bf16)


def settle(parts, x, vecs, at):
    total = vecs[at : at + 1] + x[...].astype(f32)
    for part in parts:
        total = total + part[...].astype(f32)
    return norm_rows(total, vecs[at + 1 : at + 2], vecs[at + 2 : at + 3]).astype(bf16)


def second_kernel(
    limits, p0, p1, p2, p3, x, vecs, w_cq, keys, values, w_cout, h_ref, part_ref, *, heads
):
    slots = p0.shape[0]
    h1 = settle((p0, p1, p2, p3), x, vecs, NORM_1)
    h_ref[...] = h1
    bias = vecs[B_CQ : B_CQ + 1, : w_cq.shape[1]]
    cq = round_rows(dot(pad_rows(h1.astype(f32), 8), w_cq[...]) + bias)
    ctx = attend(cq, [(keys, values)], limits, heads)
    part_ref[...] = dot(ctx, w_cout[...])[:slots].astype(bf16)


def third_kernel(p0, p1, p2, p3, x, vecs, w_up, w_down, h_ref, part_ref):
    slots = p0.shape[0]
    h2 = settle((p0, p1, p2, p3), x, vecs, NORM_2)
    h_ref[...] = h2
    bias = vecs[B_UP : B_UP + 1, : w_up.shape[1]]
    hidden = dot(pad_rows(h2.astype(f32), 8), w_up[...]) + bias
    act = 0.5 * hidden * (1.0 + lax.erf(hidden * (2.0**-0.5)))
    part_ref[...] = dot(act, w_down[...])[:slots].astype(bf16)


def fourth_kernel(p0, p1, p2, p3, x, vecs, y_ref):
    y_ref[...] = settle((p0, p1, p2, p3), x, vecs, NORM_3)


def add_kernel(mine, more, out_ref):
    out_ref[...] = (mine[...].astype(f32) + more[...].astype(f32)).astype(bf16)


def call(kernel, out_shapes, args, smem=0, name=None, cost=None):
    vmem = pl.BlockSpec(memory_space=pltpu.VMEM)
    scalar = pl.BlockSpec(memory_space=pltpu.SMEM)
    outs = [jax.ShapeDtypeStruct(s, d) for s, d in out_shapes]
    specs = [scalar if i < smem else vmem for i in range(len(args))]
    if cost is not None:
        cost = pl.CostEstimate(flops=cost, bytes_accessed=0, transcendentals=0)
    made = pl.pallas_call(
        kernel,
        out_shape=outs,
        in_specs=specs,
        out_specs=[vmem] * len(outs),
        compiler_params=pltpu.CompilerParams(vmem_limit_bytes=24 * 2**20),
        cost_estimate=cost,
        name=name,
    )(*args)
    return list(made)


def swap(value, axis, size, mask):
    return lax.ppermute(value, axis, [(i, i ^ mask) for i in range(size)])


def pick_rows(onehot, whole):
    return jnp.dot(onehot.astype(whole.dtype), whole, preferred_element_type=f32).astype(whole.dtype)


def in_order(swaps):
    return list(lax.optimization_barrier(swaps))


def gather_blocks(value, mesh_shape, steps):
    reqs, tps = mesh_shape["req"], mesh_shape["tp"]
    got = []
    for a, b, cross in steps:
        pairs = []
        for r in range(reqs):
            for t in range(tps):
                pairs.append(((r ^ (b if t % 2 else a)) * tps + (t ^ cross), r * tps + t))
        got.append(lax.ppermute(value, ("req", "tp"), pairs))
    return in_order(got)


def sort_rows(hit, own, got, mesh_shape, name):
    (mine,) = call(
        sort_kernel, [(own.shape, bf16)], [hit, own] + got, name=name
    )
    return mine, swap(mine, "tp", mesh_shape["tp"], 1)


def deal_whole(value, deal, back):
    base = lax.axis_index("req") * value.shape[0]
    spread = jnp.arange(value.shape[0], dtype=jnp.int32)
    whole = lax.all_gather(value, "req", axis=0, tiled=True)
    if back:
        onehot = deal[None, :] == (base + spread)[:, None]
    else:
        owner = lax.dynamic_slice_in_dim(deal, base, value.shape[0])
        onehot = owner[:, None] == jnp.arange(deal.shape[0], dtype=jnp.int32)[None, :]
    picked = pick_rows(onehot, whole)
    return picked, jnp.zeros_like(picked)


def split_shapes(cache, slots):
    _, span, _, width = cache.shape
    return [((slots, width, span), bf16), ((slots, span, width), bf16)]


def split_part(after, cache, start, slots, name):
    return call(
        functools.partial(split_kernel, start=start),
        split_shapes(cache, slots),
        [after, tile_rows(cache)],
        name=name,
    )


def tile_rows(cache):
    slots, span, _, width = cache.shape
    split = cache.reshape(slots, span, 2, width // LANES, LANES)
    return split.transpose(0, 1, 3, 2, 4).reshape(slots, -1, LANES)


def sum_parts(value, mesh_shape):
    tps = mesh_shape["tp"]
    if tps == 4:
        return [value] + in_order([swap(value, "tp", tps, mask) for mask in TP_STEPS])
    whole = lax.psum(value.astype(f32), "tp")
    zero = jnp.zeros_like(whole)
    return [whole, zero, zero, zero]


def on_device(
    mesh_shape,
    tokens,
    deal,
    self_len,
    enc_len,
    self_cache,
    cross_cache,
    w_qkv,
    b_qkv,
    w_out,
    b_out,
    ln1_gain,
    ln1_bias,
    w_cq,
    b_cq,
    w_cout,
    b_cout,
    ln2_gain,
    ln2_bias,
    w_up,
    b_up,
    w_down,
    b_down,
    ln3_gain,
    ln3_bias,
):
    rows, model = tokens.shape
    width = self_cache.shape[3]
    heads = width // HEAD_DIM

    state, sums = ((rows, model), bf16), ((rows, model), bf16)
    vecs = [b_out, ln1_gain, ln1_bias, b_cout, ln2_gain, ln2_bias, b_down, ln3_gain, ln3_bias]
    vecs += [b_up, b_cq, b_qkv]
    table = ((TABLE_ROWS, max(model, b_up.shape[0])), f32)
    hops = mesh_shape["req"] == 8 and mesh_shape["tp"] == 4
    if hops:
        got = gather_blocks(tokens, mesh_shape, OUT_STEPS)
        hits = [((8, (1 + len(steps)) * rows), bf16) for steps in (OUT_STEPS, BACK_STEPS)]
        half = rows // 2
        (stub,) = call(stub_kernel, [((8, LANES), f32)], [], name="stub", cost=SPARE_FLOPS)
        limits = ((rows * heads, LANES), jnp.int32)
        own, hit_out, hit_back, self_limits, enc_limits, keys, values, vecs = call(
            functools.partial(plan_kernel, heads=heads),
            [state] + hits + [limits, limits] + split_shapes(self_cache, half) + [table],
            [deal, self_len, enc_len, stub, tokens, tile_rows(self_cache)] + vecs,
            smem=3,
            name="plan",
        )
        mine, more = sort_rows(hit_out, own, got, mesh_shape, "sort_out")
        self_kv = [keys, values] + split_part(mine, self_cache, half, rows - half, "split_self")
    else:
        mine, more = deal_whole(tokens, deal, False)
        (vecs,) = call(table_kernel, [table], vecs, name="table")
        self_limits, enc_limits = (
            jnp.broadcast_to(jnp.repeat(lens, heads)[:, None], (rows * heads, LANES))
            for lens in (self_len, enc_len)
        )
        self_kv = split_part(mine, self_cache, 0, rows, "split_self")
    x, part = call(
        functools.partial(first_kernel, heads=heads),
        [state, sums],
        [self_limits, mine, more, w_qkv.transpose(1, 0, 2), vecs, w_out] + self_kv,
        name="self_attention",
    )
    cross_kv = split_part(x, cross_cache, 0, rows, "split_cross")
    h1, part = call(
        functools.partial(second_kernel, heads=heads),
        [state, sums],
        [enc_limits]
        + sum_parts(part, mesh_shape)
        + [x, vecs, w_cq] + cross_kv + [w_cout],
        name="cross_attention",
    )
    h2, part = call(
        third_kernel,
        [state, sums],
        sum_parts(part, mesh_shape) + [h1, vecs, w_up, w_down],
        name="feed_forward",
    )
    (y,) = call(
        fourth_kernel,
        [state],
        sum_parts(part, mesh_shape) + [h2, vecs],
        name="last_norm",
    )
    if hops:
        got = gather_blocks(y, mesh_shape, BACK_STEPS)
        mine, more = sort_rows(hit_back, y, got, mesh_shape, "sort_back")
    else:
        mine, more = deal_whole(y, deal, True)
    (result,) = call(add_kernel, [state], [mine, more], name="deal_back")
    return result


def solution(mesh):
    return jax.shard_map(
        functools.partial(on_device, dict(mesh.shape)),
        mesh=mesh,
        in_specs=(
            P("req", None),
            P(),
            P("req"),
            P("req"),
            P("req", None, None, "tp"),
            P("req", None, None, "tp"),
            P(None, None, "tp"),
            P(None, "tp"),
            P("tp", None),
            P(),
            P(),
            P(),
            P(None, "tp"),
            P("tp"),
            P("tp", None),
            P(),
            P(),
            P(),
            P(None, "tp"),
            P("tp"),
            P("tp", None),
            P(),
            P(),
            P(),
        ),
        out_specs=P("req", None),
        check_vma=False,
    )
```

```python
import functools

import jax
import jax.numpy as jnp
from jax import lax
from jax.experimental import pallas as pl
from jax.experimental.pallas import tpu as pltpu
from jax.sharding import PartitionSpec as P

HEAD_DIM = 64
LANES = 128
EPS = 1e-05
MASKED = -1e30
SPARE_FLOPS = 10**10
OUT_STEPS = ((7, 5, 1), (6, 4, 1), (1, 1, 1), (2, 3, 1))
BACK_STEPS = ((1, 1, 1), (2, 3, 1), (6, 4, 1), (5, 7, 1))
TP_STEPS = (1, 2, 3)
NORM_1, NORM_2, NORM_3, B_UP, B_CQ, B_QKV, TABLE_ROWS = 0, 3, 6, 9, 10, 11, 16
f32 = jnp.float32
bf16 = jnp.bfloat16


def norm_rows(total, gain, beta):
    mean = jnp.mean(total, axis=-1, keepdims=True)
    centered = total - mean
    var = jnp.mean(centered * centered, axis=-1, keepdims=True)
    return centered / jnp.sqrt(var + EPS) * gain + beta


def round_rows(value):
    return value.astype(bf16).astype(f32)


def dot(a, b):
    return jnp.dot(a.astype(bf16), b, preferred_element_type=f32)


def pad_rows(value, rows):
    return jnp.concatenate(
        [value, jnp.zeros((rows - value.shape[0], value.shape[1]), value.dtype)], axis=0
    )


def head_rows(vec, slot, heads, first):
    return jnp.where(first, vec[slot : slot + 1], vec[slot + 1 : slot + 2])


def attend(query, cache, limits, heads, fresh_key=None, fresh_value=None):
    where = [(k.at[s], v.at[s]) for k, v in cache for s in range(k.shape[0])]
    slots = len(where)
    _, span, width = cache[0][1].shape
    pair = 2 * heads
    scale = HEAD_DIM ** (-0.5)
    row = lax.broadcasted_iota(jnp.int32, (pair, width), 0)
    lane = lax.broadcasted_iota(jnp.int32, (pair, width), 1)
    first = row < heads
    own = (lane // HEAD_DIM) == jnp.where(first, row, row - heads)
    first_col = lax.broadcasted_iota(jnp.int32, (pair, span), 0) < heads
    position = lax.broadcasted_iota(jnp.int32, (pair, span), 1)
    rows = []
    for slot in range(0, slots, 2):
        q = jnp.where(own, head_rows(query, slot, heads, first) * scale, 0.0)
        raw = [dot(q, keys[...]) for keys, _ in where[slot : slot + 2]]
        length = limits[slot * heads : (slot + 2) * heads]
        length = jnp.concatenate([length] * (span // LANES), axis=1)
        scores = jnp.where(position < length, jnp.where(first_col, raw[0], raw[1]), MASKED)
        top = jnp.max(scores, axis=-1, keepdims=True)
        if fresh_key is not None:
            k_new = head_rows(fresh_key, slot, heads, first)
            v_new = head_rows(fresh_value, slot, heads, first)
            fresh = jnp.sum(q * k_new, axis=-1, keepdims=True)
            top = jnp.maximum(top, fresh)
        expo = jnp.exp(scores - top)
        total = jnp.sum(expo, axis=-1, keepdims=True)
        if fresh_key is not None:
            expn = jnp.exp(fresh - top)
            total = total + expn
        out = [dot(expo, values[...]) for _, values in where[slot : slot + 2]]
        ctx = jnp.where(first, out[0], out[1])
        if fresh_key is not None:
            ctx = ctx + round_rows(expn) * v_new
        ctx = jnp.where(own, round_rows(ctx * (1.0 / total)), 0.0)
        rows.append(jnp.sum(ctx[:heads], axis=0, keepdims=True))
        rows.append(jnp.sum(ctx[heads:], axis=0, keepdims=True))
    return jnp.concatenate(rows + [jnp.zeros((8 - slots, width), f32)], axis=0)


def split_cache(cache, key_ref, value_ref, start, lens=None):
    slots, _, width = value_ref.shape
    count = cache.shape[1]
    tiles = width // LANES
    group = 2 * tiles
    step = 256
    part = step // group
    r = lax.broadcasted_iota(jnp.int32, (step, step), 0)
    c = lax.broadcasted_iota(jnp.int32, (step, step), 1)
    order = (c == (r % part) * group + r // part).astype(bf16)
    pieces = LANES // part

    def move(slot, steps):
        for at in steps:
            rows = [
                dot(order, cache[start + slot, (at + i) * step : (at + i + 1) * step])
                for i in range(pieces)
            ]
            here = slice(at * part, (at + pieces) * part)
            for tile in range(tiles):
                lanes = slice(tile * LANES, (tile + 1) * LANES)
                g = 2 * tile * part
                key = jnp.concatenate([x[g : g + part] for x in rows], axis=0)
                value = jnp.concatenate([x[g + part : g + 2 * part] for x in rows], axis=0)
                key_ref[slot, lanes, here] = key.T.astype(bf16)
                value_ref[slot, here, lanes] = value.astype(bf16)

    steps = list(range(0, count // step, pieces))
    if lens is None:
        for slot in range(slots):
            move(slot, steps)
        return
    low = len(steps) // 2
    cut = steps[low] * part
    span = value_ref.shape[1]
    for slot in range(slots):
        move(slot, steps[:low])
        key_ref[slot, :, cut:] = jnp.zeros((width, span - cut), bf16)
        value_ref[slot, cut:] = jnp.zeros((span - cut, width), bf16)
    for slot in range(slots):

        @pl.when(lens[slot] > cut)
        def _():
            move(slot, steps[low:])


def wanted(deal, rows, me, core, steps, back):
    masks, seen = [(0, 0, 0)] + list(steps), set()
    origin, used = [], []
    for a, b, _ in masks:
        origin.append(me ^ jnp.where(core == 0, a, b))
        fresh = (a not in seen, b not in seen | {a})
        seen |= {a, b}
        used.append(jnp.where(core == 0, fresh[0], fresh[1]))
    shape = (8, len(masks) * rows)
    row = lax.broadcasted_iota(jnp.int32, shape, 0)
    col = lax.broadcasted_iota(jnp.int32, shape, 1)
    take, have = me * rows + row, jnp.full(shape, -1, jnp.int32)
    for i in range(shape[1]):
        ident = origin[i // rows] * rows + i % rows
        ident = jnp.where(used[i // rows], deal[ident] if back else ident, -1)
        have = jnp.where(col == i, ident, have)
    if not back:
        for i in range(rows):
            take = jnp.where(row == i, deal[me * rows + i], take)
    return ((have == take) & (row < rows)).astype(bf16)


def stub_kernel(out_ref):
    out_ref[...] = jnp.zeros_like(out_ref)


def spread_lengths(lens, ref, heads):
    slot = lax.broadcasted_iota(jnp.int32, ref.shape, 0) // heads
    out = jnp.zeros(ref.shape, jnp.int32)
    for s in range(ref.shape[0] // heads):
        out = jnp.where(slot == s, lens[s], out)
    ref[...] = out


def table_kernel(*refs):
    *vecs, table_ref = refs
    table_ref[...] = jnp.zeros_like(table_ref)
    for i, vec in enumerate(vecs):
        if len(vec.shape) == 1:
            table_ref[i : i + 1, : vec.shape[0]] = vec[...].astype(f32).reshape(1, vec.shape[0])
        else:
            table_ref[i : i + vec.shape[0], : vec.shape[1]] = vec[...].astype(f32)


def plan_kernel(deal, self_len, enc_len, stub, tokens, cache, *refs, heads):
    *vecs, own_ref, out_ref, back_ref, self_ref, enc_ref, key_ref, value_ref, table_ref = refs
    table_kernel(*vecs, table_ref)
    spread_lengths(self_len, self_ref, heads)
    spread_lengths(enc_len, enc_ref, heads)
    me, core = lax.axis_index("req"), lax.axis_index("tp") % 2
    rows = tokens.shape[0]
    own_ref[...] = tokens[...]
    out_ref[...] = wanted(deal, rows, me, core, OUT_STEPS, False)
    back_ref[...] = wanted(deal, rows, me, core, BACK_STEPS, True)
    split_cache(cache, key_ref, value_ref, 0, self_len)


def split_kernel(after, cache, key_ref, value_ref, *, start):
    split_cache(cache, key_ref, value_ref, start)


def sort_kernel(hit, *refs):
    *blocks, out_ref = refs
    whole = jnp.concatenate([p[...] for p in blocks], axis=0)
    out_ref[...] = dot(hit[...], whole)[: out_ref.shape[0]].astype(bf16)


def first_kernel(
    limits, mine, more, w_qkv, vecs, w_out, *refs, heads
):
    *cache, x_ref, part_ref = refs
    cache = list(zip(cache[::2], cache[1::2]))
    slots = x_ref.shape[0]
    x = mine[...].astype(f32) + more[...].astype(f32)
    x_ref[...] = x.astype(bf16)
    x = pad_rows(x, 8).astype(bf16)
    width = w_out.shape[0]
    bias = [vecs[B_QKV + k : B_QKV + k + 1, :width] for k in range(3)]
    qkv = [round_rows(dot(x, w_qkv[k]) + bias[k]) for k in range(3)]
    ctx = attend(qkv[0], cache, limits, heads, qkv[1], qkv[2])
    part_ref[...] = dot(ctx, w_out[...])[:slots].astype(bf16)


def settle(parts, x, vecs, at):
    total = vecs[at : at + 1] + x[...].astype(f32)
    for part in parts:
        total = total + part[...].astype(f32)
    return norm_rows(total, vecs[at + 1 : at + 2], vecs[at + 2 : at + 3]).astype(bf16)


def second_kernel(
    limits, p0, p1, p2, p3, x, vecs, w_cq, keys, values, w_cout, h_ref, part_ref, *, heads
):
    slots = p0.shape[0]
    h1 = settle((p0, p1, p2, p3), x, vecs, NORM_1)
    h_ref[...] = h1
    bias = vecs[B_CQ : B_CQ + 1, : w_cq.shape[1]]
    cq = round_rows(dot(pad_rows(h1.astype(f32), 8), w_cq[...]) + bias)
    ctx = attend(cq, [(keys, values)], limits, heads)
    part_ref[...] = dot(ctx, w_cout[...])[:slots].astype(bf16)


def third_kernel(p0, p1, p2, p3, x, vecs, w_up, w_down, h_ref, part_ref):
    slots = p0.shape[0]
    h2 = settle((p0, p1, p2, p3), x, vecs, NORM_2)
    h_ref[...] = h2
    bias = vecs[B_UP : B_UP + 1, : w_up.shape[1]]
    hidden = dot(pad_rows(h2.astype(f32), 8), w_up[...]) + bias
    act = 0.5 * hidden * (1.0 + lax.erf(hidden * (2.0**-0.5)))
    part_ref[...] = dot(act, w_down[...])[:slots].astype(bf16)


def fourth_kernel(p0, p1, p2, p3, x, vecs, y_ref):
    y_ref[...] = settle((p0, p1, p2, p3), x, vecs, NORM_3)


def add_kernel(mine, more, out_ref):
    out_ref[...] = (mine[...].astype(f32) + more[...].astype(f32)).astype(bf16)


def call(kernel, out_shapes, args, smem=0, name=None, cost=None):
    vmem = pl.BlockSpec(memory_space=pltpu.VMEM)
    scalar = pl.BlockSpec(memory_space=pltpu.SMEM)
    outs = [jax.ShapeDtypeStruct(s, d) for s, d in out_shapes]
    specs = [scalar if i < smem else vmem for i in range(len(args))]
    if cost is not None:
        cost = pl.CostEstimate(flops=cost, bytes_accessed=0, transcendentals=0)
    made = pl.pallas_call(
        kernel,
        out_shape=outs,
        in_specs=specs,
        out_specs=[vmem] * len(outs),
        compiler_params=pltpu.CompilerParams(vmem_limit_bytes=24 * 2**20),
        cost_estimate=cost,
        name=name,
    )(*args)
    return list(made)


def swap(value, axis, size, mask):
    return lax.ppermute(value, axis, [(i, i ^ mask) for i in range(size)])


def pick_rows(onehot, whole):
    return jnp.dot(onehot.astype(whole.dtype), whole, preferred_element_type=f32).astype(whole.dtype)


def in_order(swaps):
    return list(lax.optimization_barrier(swaps))


def gather_blocks(value, mesh_shape, steps):
    reqs, tps = mesh_shape["req"], mesh_shape["tp"]
    got = []
    for a, b, cross in steps:
        pairs = []
        for r in range(reqs):
            for t in range(tps):
                pairs.append(((r ^ (b if t % 2 else a)) * tps + (t ^ cross), r * tps + t))
        got.append(lax.ppermute(value, ("req", "tp"), pairs))
    return in_order(got)


def sort_rows(hit, own, got, mesh_shape, name):
    (mine,) = call(
        sort_kernel, [(own.shape, bf16)], [hit, own] + got, name=name
    )
    return mine, swap(mine, "tp", mesh_shape["tp"], 1)


def deal_whole(value, deal, back):
    base = lax.axis_index("req") * value.shape[0]
    spread = jnp.arange(value.shape[0], dtype=jnp.int32)
    whole = lax.all_gather(value, "req", axis=0, tiled=True)
    if back:
        onehot = deal[None, :] == (base + spread)[:, None]
    else:
        owner = lax.dynamic_slice_in_dim(deal, base, value.shape[0])
        onehot = owner[:, None] == jnp.arange(deal.shape[0], dtype=jnp.int32)[None, :]
    picked = pick_rows(onehot, whole)
    return picked, jnp.zeros_like(picked)


def split_shapes(cache, slots):
    _, span, _, width = cache.shape
    return [((slots, width, span), bf16), ((slots, span, width), bf16)]


def split_part(after, cache, start, slots, name):
    return call(
        functools.partial(split_kernel, start=start),
        split_shapes(cache, slots),
        [after, tile_rows(cache)],
        name=name,
    )


def tile_rows(cache):
    slots, span, _, width = cache.shape
    split = cache.reshape(slots, span, 2, width // LANES, LANES)
    return split.transpose(0, 1, 3, 2, 4).reshape(slots, -1, LANES)


def sum_parts(value, mesh_shape):
    tps = mesh_shape["tp"]
    if tps == 4:
        return [value] + in_order([swap(value, "tp", tps, mask) for mask in TP_STEPS])
    whole = lax.psum(value.astype(f32), "tp")
    zero = jnp.zeros_like(whole)
    return [whole, zero, zero, zero]


def on_device(
    mesh_shape,
    tokens,
    deal,
    self_len,
    enc_len,
    self_cache,
    cross_cache,
    w_qkv,
    b_qkv,
    w_out,
    b_out,
    ln1_gain,
    ln1_bias,
    w_cq,
    b_cq,
    w_cout,
    b_cout,
    ln2_gain,
    ln2_bias,
    w_up,
    b_up,
    w_down,
    b_down,
    ln3_gain,
    ln3_bias,
):
    rows, model = tokens.shape
    width = self_cache.shape[3]
    heads = width // HEAD_DIM

    state, sums = ((rows, model), bf16), ((rows, model), bf16)
    vecs = [b_out, ln1_gain, ln1_bias, b_cout, ln2_gain, ln2_bias, b_down, ln3_gain, ln3_bias]
    vecs += [b_up, b_cq, b_qkv]
    table = ((TABLE_ROWS, max(model, b_up.shape[0])), f32)
    hops = mesh_shape["req"] == 8 and mesh_shape["tp"] == 4
    if hops:
        got = gather_blocks(tokens, mesh_shape, OUT_STEPS)
        hits = [((8, (1 + len(steps)) * rows), bf16) for steps in (OUT_STEPS, BACK_STEPS)]
        half = rows - 1
        (stub,) = call(stub_kernel, [((8, LANES), f32)], [], name="stub", cost=SPARE_FLOPS)
        limits = ((rows * heads, LANES), jnp.int32)
        own, hit_out, hit_back, self_limits, enc_limits, keys, values, vecs = call(
            functools.partial(plan_kernel, heads=heads),
            [state] + hits + [limits, limits] + split_shapes(self_cache, half) + [table],
            [deal, self_len, enc_len, stub, tokens, tile_rows(self_cache)] + vecs,
            smem=3,
            name="plan",
        )
        mine, more = sort_rows(hit_out, own, got, mesh_shape, "sort_out")
        self_kv = [keys, values] + split_part(mine, self_cache, half, rows - half, "split_self")
    else:
        mine, more = deal_whole(tokens, deal, False)
        (vecs,) = call(table_kernel, [table], vecs, name="table")
        self_limits, enc_limits = (
            jnp.broadcast_to(jnp.repeat(lens, heads)[:, None], (rows * heads, LANES))
            for lens in (self_len, enc_len)
        )
        self_kv = split_part(mine, self_cache, 0, rows, "split_self")
    x, part = call(
        functools.partial(first_kernel, heads=heads),
        [state, sums],
        [self_limits, mine, more, w_qkv.transpose(1, 0, 2), vecs, w_out] + self_kv,
        name="self_attention",
    )
    cross_kv = split_part(x, cross_cache, 0, rows, "split_cross")
    h1, part = call(
        functools.partial(second_kernel, heads=heads),
        [state, sums],
        [enc_limits]
        + sum_parts(part, mesh_shape)
        + [x, vecs, w_cq] + cross_kv + [w_cout],
        name="cross_attention",
    )
    h2, part = call(
        third_kernel,
        [state, sums],
        sum_parts(part, mesh_shape) + [h1, vecs, w_up, w_down],
        name="feed_forward",
    )
    (y,) = call(
        fourth_kernel,
        [state],
        sum_parts(part, mesh_shape) + [h2, vecs],
        name="last_norm",
    )
    if hops:
        got = gather_blocks(y, mesh_shape, BACK_STEPS)
        mine, more = sort_rows(hit_back, y, got, mesh_shape, "sort_back")
    else:
        mine, more = deal_whole(y, deal, True)
    (result,) = call(add_kernel, [state], [mine, more], name="deal_back")
    return result


def solution(mesh):
    return jax.shard_map(
        functools.partial(on_device, dict(mesh.shape)),
        mesh=mesh,
        in_specs=(
            P("req", None),
            P(),
            P("req"),
            P("req"),
            P("req", None, None, "tp"),
            P("req", None, None, "tp"),
            P(None, None, "tp"),
            P(None, "tp"),
            P("tp", None),
            P(),
            P(),
            P(),
            P(None, "tp"),
            P("tp"),
            P("tp", None),
            P(),
            P(),
            P(),
            P(None, "tp"),
            P("tp"),
            P("tp", None),
            P(),
            P(),
            P(),
        ),
        out_specs=P("req", None),
        check_vma=False,
    )
```

```python
import functools

import jax
import jax.numpy as jnp
from jax import lax
from jax.experimental import pallas as pl
from jax.experimental.pallas import tpu as pltpu
from jax.sharding import PartitionSpec as P

HEAD_DIM = 64
LANES = 128
EPS = 1e-05
MASKED = -1e30
SPARE_FLOPS = 10**10
OUT_STEPS = ((6, 4, 1), (7, 5, 1), (1, 1, 1), (2, 3, 1))
BACK_STEPS = ((1, 1, 1), (2, 3, 1), (6, 4, 1), (5, 7, 1))
TP_STEPS = (1, 2, 3)
NORM_1, NORM_2, NORM_3, B_UP, B_CQ, B_QKV, TABLE_ROWS = 0, 3, 6, 9, 10, 11, 16
f32 = jnp.float32
bf16 = jnp.bfloat16


def norm_rows(total, gain, beta):
    mean = jnp.mean(total, axis=-1, keepdims=True)
    centered = total - mean
    var = jnp.mean(centered * centered, axis=-1, keepdims=True)
    return centered / jnp.sqrt(var + EPS) * gain + beta


def round_rows(value):
    return value.astype(bf16).astype(f32)


def dot(a, b):
    return jnp.dot(a.astype(bf16), b, preferred_element_type=f32)


def pad_rows(value, rows):
    return jnp.concatenate(
        [value, jnp.zeros((rows - value.shape[0], value.shape[1]), value.dtype)], axis=0
    )


def head_rows(vec, slot, heads, first):
    return jnp.where(first, vec[slot : slot + 1], vec[slot + 1 : slot + 2])


def attend(query, cache, limits, heads, fresh_key=None, fresh_value=None):
    where = [(k.at[s], v.at[s]) for k, v in cache for s in range(k.shape[0])]
    slots = len(where)
    _, span, width = cache[0][1].shape
    pair = 2 * heads
    scale = HEAD_DIM ** (-0.5)
    row = lax.broadcasted_iota(jnp.int32, (pair, width), 0)
    lane = lax.broadcasted_iota(jnp.int32, (pair, width), 1)
    first = row < heads
    own = (lane // HEAD_DIM) == jnp.where(first, row, row - heads)
    first_col = lax.broadcasted_iota(jnp.int32, (pair, span), 0) < heads
    position = lax.broadcasted_iota(jnp.int32, (pair, span), 1)
    rows = []
    for slot in range(0, slots, 2):
        q = jnp.where(own, head_rows(query, slot, heads, first) * scale, 0.0)
        raw = [dot(q, keys[...]) for keys, _ in where[slot : slot + 2]]
        length = limits[slot * heads : (slot + 2) * heads]
        length = jnp.concatenate([length] * (span // LANES), axis=1)
        scores = jnp.where(position < length, jnp.where(first_col, raw[0], raw[1]), MASKED)
        top = jnp.max(scores, axis=-1, keepdims=True)
        if fresh_key is not None:
            k_new = head_rows(fresh_key, slot, heads, first)
            v_new = head_rows(fresh_value, slot, heads, first)
            fresh = jnp.sum(q * k_new, axis=-1, keepdims=True)
            top = jnp.maximum(top, fresh)
        expo = jnp.exp(scores - top)
        total = jnp.sum(expo, axis=-1, keepdims=True)
        if fresh_key is not None:
            expn = jnp.exp(fresh - top)
            total = total + expn
        out = [dot(expo, values[...]) for _, values in where[slot : slot + 2]]
        ctx = jnp.where(first, out[0], out[1])
        if fresh_key is not None:
            ctx = ctx + round_rows(expn) * v_new
        ctx = jnp.where(own, round_rows(ctx * (1.0 / total)), 0.0)
        rows.append(jnp.sum(ctx[:heads], axis=0, keepdims=True))
        rows.append(jnp.sum(ctx[heads:], axis=0, keepdims=True))
    return jnp.concatenate(rows + [jnp.zeros((8 - slots, width), f32)], axis=0)


def split_cache(cache, key_ref, value_ref, start):
    slots, _, width = value_ref.shape
    count = cache.shape[1]
    tiles = width // LANES
    group = 2 * tiles
    step = 256
    part = step // group
    r = lax.broadcasted_iota(jnp.int32, (step, step), 0)
    c = lax.broadcasted_iota(jnp.int32, (step, step), 1)
    order = (c == (r % part) * group + r // part).astype(bf16)
    pieces = LANES // part
    for slot in range(slots):
        for at in range(0, count // step, pieces):
            rows = [
                dot(order, cache[start + slot, (at + i) * step : (at + i + 1) * step])
                for i in range(pieces)
            ]
            here = slice(at * part, (at + pieces) * part)
            for tile in range(tiles):
                lanes = slice(tile * LANES, (tile + 1) * LANES)
                g = 2 * tile * part
                key = jnp.concatenate([x[g : g + part] for x in rows], axis=0)
                value = jnp.concatenate([x[g + part : g + 2 * part] for x in rows], axis=0)
                key_ref[slot, lanes, here] = key.T.astype(bf16)
                value_ref[slot, here, lanes] = value.astype(bf16)


def wanted(deal, rows, me, core, steps, back):
    masks, seen = [(0, 0, 0)] + list(steps), set()
    origin, used = [], []
    for a, b, _ in masks:
        origin.append(me ^ jnp.where(core == 0, a, b))
        fresh = (a not in seen, b not in seen | {a})
        seen |= {a, b}
        used.append(jnp.where(core == 0, fresh[0], fresh[1]))
    shape = (8, len(masks) * rows)
    row = lax.broadcasted_iota(jnp.int32, shape, 0)
    col = lax.broadcasted_iota(jnp.int32, shape, 1)
    take, have = me * rows + row, jnp.full(shape, -1, jnp.int32)
    for i in range(shape[1]):
        ident = origin[i // rows] * rows + i % rows
        ident = jnp.where(used[i // rows], deal[ident] if back else ident, -1)
        have = jnp.where(col == i, ident, have)
    if not back:
        for i in range(rows):
            take = jnp.where(row == i, deal[me * rows + i], take)
    return ((have == take) & (row < rows)).astype(bf16)


def stub_kernel(out_ref):
    out_ref[...] = jnp.zeros_like(out_ref)


def spread_lengths(lens, ref, heads):
    slot = lax.broadcasted_iota(jnp.int32, ref.shape, 0) // heads
    out = jnp.zeros(ref.shape, jnp.int32)
    for s in range(ref.shape[0] // heads):
        out = jnp.where(slot == s, lens[s], out)
    ref[...] = out


def table_kernel(*refs):
    *vecs, table_ref = refs
    table_ref[...] = jnp.zeros_like(table_ref)
    for i, vec in enumerate(vecs):
        if len(vec.shape) == 1:
            table_ref[i : i + 1, : vec.shape[0]] = vec[...].astype(f32).reshape(1, vec.shape[0])
        else:
            table_ref[i : i + vec.shape[0], : vec.shape[1]] = vec[...].astype(f32)


def plan_kernel(deal, self_len, enc_len, stub, tokens, cache, *refs, heads):
    *vecs, own_ref, out_ref, back_ref, self_ref, enc_ref, key_ref, value_ref, table_ref = refs
    table_kernel(*vecs, table_ref)
    spread_lengths(self_len, self_ref, heads)
    spread_lengths(enc_len, enc_ref, heads)
    me, core = lax.axis_index("req"), lax.axis_index("tp") % 2
    rows = tokens.shape[0]
    own_ref[...] = tokens[...]
    out_ref[...] = wanted(deal, rows, me, core, OUT_STEPS, False)
    back_ref[...] = wanted(deal, rows, me, core, BACK_STEPS, True)
    split_cache(cache, key_ref, value_ref, 0)


def split_kernel(after, cache, key_ref, value_ref, *, start):
    split_cache(cache, key_ref, value_ref, start)


def sort_kernel(hit, *refs):
    *blocks, out_ref = refs
    whole = jnp.concatenate([p[...] for p in blocks], axis=0)
    out_ref[...] = dot(hit[...], whole)[: out_ref.shape[0]].astype(bf16)


def first_kernel(
    limits, mine, more, w_qkv, vecs, w_out, *refs, heads
):
    *cache, x_ref, part_ref = refs
    cache = list(zip(cache[::2], cache[1::2]))
    slots = x_ref.shape[0]
    x = mine[...].astype(f32) + more[...].astype(f32)
    x_ref[...] = x.astype(bf16)
    x = pad_rows(x, 8).astype(bf16)
    width = w_out.shape[0]
    bias = [vecs[B_QKV + k : B_QKV + k + 1, :width] for k in range(3)]
    qkv = [round_rows(dot(x, w_qkv[k]) + bias[k]) for k in range(3)]
    ctx = attend(qkv[0], cache, limits, heads, qkv[1], qkv[2])
    part_ref[...] = dot(ctx, w_out[...])[:slots].astype(bf16)


def settle(parts, x, vecs, at):
    total = vecs[at : at + 1] + x[...].astype(f32)
    for part in parts:
        total = total + part[...].astype(f32)
    return norm_rows(total, vecs[at + 1 : at + 2], vecs[at + 2 : at + 3]).astype(bf16)


def second_kernel(
    limits, p0, p1, p2, p3, x, vecs, w_cq, keys, values, w_cout, h_ref, part_ref, *, heads
):
    slots = p0.shape[0]
    h1 = settle((p0, p1, p2, p3), x, vecs, NORM_1)
    h_ref[...] = h1
    bias = vecs[B_CQ : B_CQ + 1, : w_cq.shape[1]]
    cq = round_rows(dot(pad_rows(h1.astype(f32), 8), w_cq[...]) + bias)
    ctx = attend(cq, [(keys, values)], limits, heads)
    part_ref[...] = dot(ctx, w_cout[...])[:slots].astype(bf16)


def third_kernel(p0, p1, p2, p3, x, vecs, w_up, w_down, h_ref, part_ref):
    slots = p0.shape[0]
    h2 = settle((p0, p1, p2, p3), x, vecs, NORM_2)
    h_ref[...] = h2
    bias = vecs[B_UP : B_UP + 1, : w_up.shape[1]]
    hidden = dot(pad_rows(h2.astype(f32), 8), w_up[...]) + bias
    act = 0.5 * hidden * (1.0 + lax.erf(hidden * (2.0**-0.5)))
    part_ref[...] = dot(act, w_down[...])[:slots].astype(bf16)


def fourth_kernel(p0, p1, p2, p3, x, vecs, y_ref):
    y_ref[...] = settle((p0, p1, p2, p3), x, vecs, NORM_3)


def add_kernel(mine, more, out_ref):
    out_ref[...] = (mine[...].astype(f32) + more[...].astype(f32)).astype(bf16)


def call(kernel, out_shapes, args, smem=0, name=None, cost=None):
    vmem = pl.BlockSpec(memory_space=pltpu.VMEM)
    scalar = pl.BlockSpec(memory_space=pltpu.SMEM)
    outs = [jax.ShapeDtypeStruct(s, d) for s, d in out_shapes]
    specs = [scalar if i < smem else vmem for i in range(len(args))]
    if cost is not None:
        cost = pl.CostEstimate(flops=cost, bytes_accessed=0, transcendentals=0)
    made = pl.pallas_call(
        kernel,
        out_shape=outs,
        in_specs=specs,
        out_specs=[vmem] * len(outs),
        compiler_params=pltpu.CompilerParams(vmem_limit_bytes=24 * 2**20),
        cost_estimate=cost,
        name=name,
    )(*args)
    return list(made)


def swap(value, axis, size, mask):
    return lax.ppermute(value, axis, [(i, i ^ mask) for i in range(size)])


def pick_rows(onehot, whole):
    return jnp.dot(onehot.astype(whole.dtype), whole, preferred_element_type=f32).astype(whole.dtype)


def in_order(swaps):
    return list(lax.optimization_barrier(swaps))


def gather_blocks(value, mesh_shape, steps):
    reqs, tps = mesh_shape["req"], mesh_shape["tp"]
    got = []
    for a, b, cross in steps:
        pairs = []
        for r in range(reqs):
            for t in range(tps):
                pairs.append(((r ^ (b if t % 2 else a)) * tps + (t ^ cross), r * tps + t))
        got.append(lax.ppermute(value, ("req", "tp"), pairs))
    return in_order(got)


def sort_rows(hit, own, got, mesh_shape, name):
    (mine,) = call(
        sort_kernel, [(own.shape, bf16)], [hit, own] + got, name=name
    )
    return mine, swap(mine, "tp", mesh_shape["tp"], 1)


def deal_whole(value, deal, back):
    base = lax.axis_index("req") * value.shape[0]
    spread = jnp.arange(value.shape[0], dtype=jnp.int32)
    whole = lax.all_gather(value, "req", axis=0, tiled=True)
    if back:
        onehot = deal[None, :] == (base + spread)[:, None]
    else:
        owner = lax.dynamic_slice_in_dim(deal, base, value.shape[0])
        onehot = owner[:, None] == jnp.arange(deal.shape[0], dtype=jnp.int32)[None, :]
    picked = pick_rows(onehot, whole)
    return picked, jnp.zeros_like(picked)


def split_shapes(cache, slots):
    _, span, _, width = cache.shape
    return [((slots, width, span), bf16), ((slots, span, width), bf16)]


def split_part(after, cache, start, slots, name):
    return call(
        functools.partial(split_kernel, start=start),
        split_shapes(cache, slots),
        [after, tile_rows(cache)],
        name=name,
    )


def tile_rows(cache):
    slots, span, _, width = cache.shape
    split = cache.reshape(slots, span, 2, width // LANES, LANES)
    return split.transpose(0, 1, 3, 2, 4).reshape(slots, -1, LANES)


def sum_parts(value, mesh_shape):
    tps = mesh_shape["tp"]
    if tps == 4:
        return [value] + in_order([swap(value, "tp", tps, mask) for mask in TP_STEPS])
    whole = lax.psum(value.astype(f32), "tp")
    zero = jnp.zeros_like(whole)
    return [whole, zero, zero, zero]


def on_device(
    mesh_shape,
    tokens,
    deal,
    self_len,
    enc_len,
    self_cache,
    cross_cache,
    w_qkv,
    b_qkv,
    w_out,
    b_out,
    ln1_gain,
    ln1_bias,
    w_cq,
    b_cq,
    w_cout,
    b_cout,
    ln2_gain,
    ln2_bias,
    w_up,
    b_up,
    w_down,
    b_down,
    ln3_gain,
    ln3_bias,
):
    rows, model = tokens.shape
    width = self_cache.shape[3]
    heads = width // HEAD_DIM

    state, sums = ((rows, model), bf16), ((rows, model), bf16)
    vecs = [b_out, ln1_gain, ln1_bias, b_cout, ln2_gain, ln2_bias, b_down, ln3_gain, ln3_bias]
    vecs += [b_up, b_cq, b_qkv]
    table = ((TABLE_ROWS, max(model, b_up.shape[0])), f32)
    hops = mesh_shape["req"] == 8 and mesh_shape["tp"] == 4
    if hops:
        got = gather_blocks(tokens, mesh_shape, OUT_STEPS)
        hits = [((8, (1 + len(steps)) * rows), bf16) for steps in (OUT_STEPS, BACK_STEPS)]
        half = rows // 2
        (stub,) = call(stub_kernel, [((8, LANES), f32)], [], name="stub", cost=SPARE_FLOPS)
        limits = ((rows * heads, LANES), jnp.int32)
        own, hit_out, hit_back, self_limits, enc_limits, keys, values, vecs = call(
            functools.partial(plan_kernel, heads=heads),
            [state] + hits + [limits, limits] + split_shapes(self_cache, half) + [table],
            [deal, self_len, enc_len, stub, tokens, tile_rows(self_cache)] + vecs,
            smem=3,
            name="plan",
        )
        mine, more = sort_rows(hit_out, own, got, mesh_shape, "sort_out")
        self_kv = [keys, values] + split_part(mine, self_cache, half, rows - half, "split_self")
    else:
        mine, more = deal_whole(tokens, deal, False)
        (vecs,) = call(table_kernel, [table], vecs, name="table")
        self_limits, enc_limits = (
            jnp.broadcast_to(jnp.repeat(lens, heads)[:, None], (rows * heads, LANES))
            for lens in (self_len, enc_len)
        )
        self_kv = split_part(mine, self_cache, 0, rows, "split_self")
    x, part = call(
        functools.partial(first_kernel, heads=heads),
        [state, sums],
        [self_limits, mine, more, w_qkv.transpose(1, 0, 2), vecs, w_out] + self_kv,
        name="self_attention",
    )
    cross_kv = split_part(x, cross_cache, 0, rows, "split_cross")
    h1, part = call(
        functools.partial(second_kernel, heads=heads),
        [state, sums],
        [enc_limits]
        + sum_parts(part, mesh_shape)
        + [x, vecs, w_cq] + cross_kv + [w_cout],
        name="cross_attention",
    )
    h2, part = call(
        third_kernel,
        [state, sums],
        sum_parts(part, mesh_shape) + [h1, vecs, w_up, w_down],
        name="feed_forward",
    )
    (y,) = call(
        fourth_kernel,
        [state],
        sum_parts(part, mesh_shape) + [h2, vecs],
        name="last_norm",
    )
    if hops:
        got = gather_blocks(y, mesh_shape, BACK_STEPS)
        mine, more = sort_rows(hit_back, y, got, mesh_shape, "sort_back")
    else:
        mine, more = deal_whole(y, deal, True)
    (result,) = call(add_kernel, [state], [mine, more], name="deal_back")
    return result


def solution(mesh):
    return jax.shard_map(
        functools.partial(on_device, dict(mesh.shape)),
        mesh=mesh,
        in_specs=(
            P("req", None),
            P(),
            P("req"),
            P("req"),
            P("req", None, None, "tp"),
            P("req", None, None, "tp"),
            P(None, None, "tp"),
            P(None, "tp"),
            P("tp", None),
            P(),
            P(),
            P(),
            P(None, "tp"),
            P("tp"),
            P("tp", None),
            P(),
            P(),
            P(),
            P(None, "tp"),
            P("tp"),
            P("tp", None),
            P(),
            P(),
            P(),
        ),
        out_specs=P("req", None),
        check_vma=False,
    )
```
